512 devices in a mesh: src: 16 (over y, core), tgt: 32 (over x, z).
Axes of the slice: x: 4, y: 8, z: 8, core: 2. Of those that a mesh axis runs over, the one named last changes fastest.
Arguments:
- src_centroids: bfloat16 [64, 16384], P(None, 'src')
- tgt_centroids: bfloat16 [64, 16384], P(None, 'tgt')
- src_weights: float32 [16384], P('src'), may hold values from -3 to 3
- tgt_weights: float32 [16384], P('tgt'), may hold values from -3 to 3
- src_cells: bfloat16 [64, 131072], P(None, 'src')
- tgt_cells: bfloat16 [64, 65536], P(None, 'tgt')
- src_mass: float32 [131072], P('src'), may hold values from -3 to 3
- tgt_mass: float32 [65536], P('tgt'), may hold values from -3 to 3
- src_cluster: int32 [131072], P('src'), may hold values from 0 to 16383
- tgt_cluster: int32 [65536], P('tgt'), may hold values from 0 to 16383
- support: int32 [512, 32, 4], P('src', 'tgt'), may hold values from 0 to 7, as said below
- counts: int32 [512, 32], P('src', 'tgt'), may hold values from 1 to 4, as said below
Outputs:
- fine_src: float32 [131072], P('src')
- fine_tgt: float32 [65536], P('tgt')
The draws below stay inside these ranges and needn't reach their ends.
Inputs may be any that keep to these rules, and one draw needn't show every extreme that they name: support[b, t, m] is a tile number local to target shard t; the entries with m < counts[b, t] are distinct, later entries are ignored; for every source shard and target shard, the live entries of the shard's 32 source blocks name every one of the 8 local tiles. `counts`: for every source shard and target shard, some block of the source shard has 4 live entries.
All inputs are finite; a program needn't handle non-finite values.
Results may differ from the reference program's by a relative error of at most 0.0003.
Values sent between devices are 32-bit elements; how exact they have to be, the bound alone decides.
No kernel may reach another device: no remote copies, remote signals or barrier semaphores. Data moves between devices by JAX's collectives and lax.ppermute only.
A program may use at most 64 MiB of HBM per device.

```python
import math
import jax
import jax.numpy as jnp
from jax import lax

E = 64
TILE = 256
MOST = 4
BLK_DEV = 32
TIL_DEV = 8
COARSE_IT = 2
FINE_IT = 2
KS = 16384
KT = 16384
NB = 512
NS = 131072
NT = 65536
N_SRC = 16
N_TGT = 32


def point_cloud(key, count, lowest, highest):
    values = jax.random.normal(jax.random.fold_in(key, 1), (E, count), jnp.float32)
    logs = jax.random.uniform(jax.random.fold_in(key, 2), (1, count), jnp.float32, math.log(lowest), math.log(highest))
    return (values * jnp.exp(logs)).astype(jnp.bfloat16)


def draw_src_centroids(key, part):
    key = jax.random.fold_in(key, 3)
    return point_cloud(key, KS, 0.7, 1.4)


def draw_tgt_centroids(key, part):
    key = jax.random.fold_in(key, 5)
    return point_cloud(key, KT, 0.7, 1.4)


def draw_src_cells(key, part):
    key = jax.random.fold_in(key, 7)
    return point_cloud(key, NS, 0.7, 1.4)


def draw_tgt_cells(key, part):
    key = jax.random.fold_in(key, 9)
    return point_cloud(key, NT, 0.7, 1.4)


def draw_counts(key, part):
    key = jax.random.fold_in(key, 21)
    level = jax.random.randint(jax.random.fold_in(key, 1), (N_SRC, 1, N_TGT), 1, MOST + 1)
    raw = jax.random.randint(jax.random.fold_in(key, 2), (N_SRC, BLK_DEV, N_TGT), 1, level + 1)
    busiest = jax.random.randint(jax.random.fold_in(key, 3), (N_SRC, 1, N_TGT), 0, BLK_DEV)
    local = jnp.arange(BLK_DEV, dtype=jnp.int32)[None, :, None]
    filled = jnp.where(local == busiest, MOST, raw)
    return filled.reshape(NB, N_TGT).astype(jnp.int32)


def shuffle_one(subkey):
    return jax.random.permutation(subkey, TIL_DEV - 1)


def draw_support(key, part):
    key = jax.random.fold_in(key, 31)
    offset = jax.random.randint(jax.random.fold_in(key, 1), (N_SRC, 1, N_TGT), 0, TIL_DEV)
    local = jnp.arange(BLK_DEV, dtype=jnp.int32)[None, :, None]
    first = ((local + offset) % TIL_DEV).reshape(NB * N_TGT, 1)
    subkeys = jax.random.split(jax.random.fold_in(key, 2), NB * N_TGT)
    shuffled = jax.vmap(shuffle_one)(subkeys).astype(jnp.int32)
    ahead = jnp.concatenate([jnp.zeros((NB * N_TGT, 1), jnp.int32), 1 + shuffled[:, :MOST - 1]], axis=1)
    listed = (first + ahead) % TIL_DEV
    return listed.reshape(NB, N_TGT, MOST).astype(jnp.int32)


def with_ends(drawn, key, smallest, largest):
    place = [jax.random.randint(jax.random.fold_in(key, axis), (), 0, length) for axis, length in enumerate(drawn.shape)]
    widest = drawn.shape.index(max(drawn.shape))
    beside = place[:widest] + [(place[widest] + 1) % drawn.shape[widest]] + place[widest + 1:]
    return drawn.at[tuple(place)].set(smallest).at[tuple(beside)].set(largest)


def steps_of(own_key, dims, cuts, low, top_value):
    loudness, own = 1.0, jax.random.fold_in(own_key, 6)
    for position, shards_of in cuts:
        heights = jnp.exp(jax.random.uniform(jax.random.fold_in(own, position), (shards_of,), jnp.float32, low / len(cuts), top_value / len(cuts)))
        loudness = loudness * jnp.repeat(heights, dims[position] // shards_of).reshape([-1 if axis == position else 1 for axis in range(len(dims))])
    return loudness


def setup_inputs(seed: int = 0) -> dict:
    seeds = jax.random.split(jax.random.key(seed), 13)
    return {
        "src_centroids": draw_src_centroids(jax.random.fold_in(seeds[12], 71), 0),
        "tgt_centroids": draw_tgt_centroids(jax.random.fold_in(seeds[12], 71), 0),
        "src_weights": jnp.clip(jax.random.uniform(seeds[2], (KS,), jnp.float32, -3.0, 3.0) * steps_of(seeds[2], (KS,), ((0, 16),), -0.4, 0.0), -3.0, 3.0),
        "tgt_weights": jnp.clip(jax.random.uniform(seeds[3], (KT,), jnp.float32, -3.0, 3.0) * steps_of(seeds[3], (KT,), ((0, 32),), -0.4, 0.0), -3.0, 3.0),
        "src_cells": draw_src_cells(jax.random.fold_in(seeds[12], 71), 0),
        "tgt_cells": draw_tgt_cells(jax.random.fold_in(seeds[12], 71), 0),
        "src_mass": jnp.clip(jax.random.uniform(seeds[6], (NS,), jnp.float32, -3.0, 3.0) * steps_of(seeds[6], (NS,), ((0, 16),), -0.4, 0.0), -3.0, 3.0),
        "tgt_mass": jnp.clip(jax.random.uniform(seeds[7], (NT,), jnp.float32, -3.0, 3.0) * steps_of(seeds[7], (NT,), ((0, 32),), -0.4, 0.0), -3.0, 3.0),
        "src_cluster": with_ends(jax.random.randint(seeds[8], (NS,), 0, KS), jax.random.fold_in(seeds[8], 1), 0, KS - 1).astype(jnp.int32),
        "tgt_cluster": with_ends(jax.random.randint(seeds[9], (NT,), 0, KT), jax.random.fold_in(seeds[9], 1), 0, KT - 1).astype(jnp.int32),
        "support": draw_support(jax.random.fold_in(seeds[12], 71), 0),
        "counts": draw_counts(jax.random.fold_in(seeds[12], 71), 0),
    }


entropy_scale = 0.0625
very_low = -1.0e30


def squared_norms(points):
    wide = points.astype(jnp.float32)
    return jnp.sum(wide * wide, axis=0)


def coarse_level(src_centroids, tgt_centroids, src_weights, tgt_weights):
    src_norm = squared_norms(src_centroids)
    tgt_norm = squared_norms(tgt_centroids)
    right = tgt_centroids.astype(jnp.float32)
    row_block = math.gcd(KS, 1024)
    block_count = KS // row_block
    coarse_src = jnp.zeros((KS,), jnp.float32)
    coarse_tgt = jnp.zeros((KT,), jnp.float32)
    for iteration in range(COARSE_IT):
        def one_block(index):
            start = (index * row_block).astype(jnp.int32)
            left = lax.dynamic_slice_in_dim(src_centroids, start, row_block, 1).astype(jnp.float32)
            left_norm = lax.dynamic_slice_in_dim(src_norm, start, row_block, 0)
            left_mass = lax.dynamic_slice_in_dim(src_weights, start, row_block, 0)
            left_pot = lax.dynamic_slice_in_dim(coarse_src, start, row_block, 0)
            inner = jnp.einsum("ex,ey->xy", left, right, precision=lax.Precision.HIGHEST)
            cost = (left_norm[:, None] + tgt_norm[None, :] - 2.0 * inner) / (2.0 * E)
            rows = tgt_weights[None, :] + (coarse_tgt[None, :] - cost) / entropy_scale
            row_peak = jnp.max(rows, axis=1)
            row_lse = row_peak + jnp.log(jnp.sum(jnp.exp(rows - row_peak[:, None]), axis=1))
            cols = left_mass[:, None] + (left_pot[:, None] - cost) / entropy_scale
            col_peak = jnp.max(cols, axis=0)
            col_total = jnp.sum(jnp.exp(cols - col_peak[None, :]), axis=0)
            return row_lse, col_peak, col_total

        row_lse, col_peak, col_total = lax.map(one_block, jnp.arange(block_count, dtype=jnp.int32))
        top = jnp.max(col_peak, axis=0)
        col_lse = top + jnp.log(jnp.sum(col_total * jnp.exp(col_peak - top[None, :]), axis=0))
        row_new = -entropy_scale * row_lse.reshape(KS)
        col_new = -entropy_scale * col_lse
        coarse_src = 0.5 * (coarse_src + row_new)
        coarse_tgt = 0.5 * (coarse_tgt + col_new)
    return coarse_src, coarse_tgt


def fine_level(src_cells, tgt_cells, src_mass, tgt_mass, support, counts, fine_src, fine_tgt):
    block_count = NS // TILE
    tile_total = NT // TILE
    listed = N_TGT * MOST
    tgt_tiles = tgt_cells.astype(jnp.float32).reshape(E, tile_total, TILE)
    tgt_norm = squared_norms(tgt_cells).reshape(tile_total, TILE)
    tgt_weight = tgt_mass.reshape(tile_total, TILE)
    src_norm = squared_norms(src_cells)
    shard_base = jnp.arange(N_TGT, dtype=jnp.int32)[None, :, None] * TIL_DEV
    tile_ids = (shard_base + support).reshape(block_count, listed).astype(jnp.int32)
    alive_all = (jnp.arange(MOST, dtype=jnp.int32)[None, None, :] < counts[:, :, None]).astype(jnp.int32).reshape(block_count, listed)
    flat_ids = tile_ids.reshape(block_count * listed)
    for iteration in range(FINE_IT):
        tgt_pot = fine_tgt.reshape(tile_total, TILE)

        def one_block(index):
            start = (index * TILE).astype(jnp.int32)
            left = lax.dynamic_slice_in_dim(src_cells, start, TILE, 1).astype(jnp.float32)
            left_norm = lax.dynamic_slice_in_dim(src_norm, start, TILE, 0)
            left_mass = lax.dynamic_slice_in_dim(src_mass, start, TILE, 0)
            left_pot = lax.dynamic_slice_in_dim(fine_src, start, TILE, 0)
            chosen = tile_ids[index]
            alive = alive_all[index] > 0
            right = tgt_tiles[:, chosen]
            inner = jnp.einsum("ex,emy->xmy", left, right, precision=lax.Precision.HIGHEST)
            cost = (left_norm[:, None, None] + tgt_norm[chosen][None, :, :] - 2.0 * inner) / (2.0 * E)
            rows = tgt_weight[chosen][None, :, :] + (tgt_pot[chosen][None, :, :] - cost) / entropy_scale
            rows = jnp.where(alive[None, :, None], rows, very_low)
            row_peak = jnp.max(rows, axis=(1, 2))
            row_lse = row_peak + jnp.log(jnp.sum(jnp.exp(rows - row_peak[:, None, None]), axis=(1, 2)))
            cols = left_mass[:, None, None] + (left_pot[:, None, None] - cost) / entropy_scale
            col_peak = jnp.max(cols, axis=0)
            col_total = jnp.sum(jnp.exp(cols - col_peak[None, :, :]), axis=0)
            col_peak = jnp.where(alive[:, None], col_peak, very_low)
            col_total = jnp.where(alive[:, None], col_total, 0.0)
            return row_lse, col_peak, col_total

        row_lse, col_peak, col_total = lax.map(one_block, jnp.arange(block_count, dtype=jnp.int32))
        pair_peak = col_peak.reshape(block_count * listed, TILE)
        pair_total = col_total.reshape(block_count * listed, TILE)
        top = jnp.full((tile_total, TILE), very_low, jnp.float32).at[flat_ids].max(pair_peak)
        total = jnp.zeros((tile_total, TILE), jnp.float32).at[flat_ids].add(pair_total * jnp.exp(pair_peak - top[flat_ids]))
        col_lse = (top + jnp.log(total)).reshape(NT)
        row_new = -entropy_scale * row_lse.reshape(NS)
        col_new = -entropy_scale * col_lse
        fine_src = 0.5 * (fine_src + row_new)
        fine_tgt = 0.5 * (fine_tgt + col_new)
    return fine_src, fine_tgt


def reference(src_centroids, tgt_centroids, src_weights, tgt_weights, src_cells, tgt_cells, src_mass, tgt_mass, src_cluster, tgt_cluster, support, counts):
    coarse_src, coarse_tgt = coarse_level(src_centroids, tgt_centroids, src_weights, tgt_weights)
    fine_src = coarse_src[src_cluster]
    fine_tgt = coarse_tgt[tgt_cluster]
    fine_src, fine_tgt = fine_level(src_cells, tgt_cells, src_mass, tgt_mass, support, counts, fine_src, fine_tgt)
    return (fine_src, fine_tgt)
```

```python
import functools
import math
import jax
import jax.numpy as jnp
from jax import lax
from jax.experimental import pallas as pl
from jax.experimental.pallas import tpu as pltpu
from jax.sharding import PartitionSpec as P

TILE = 256
LANES = 128
HALVES = TILE // LANES
UNROLL = 4

eps = 0.0625
log2e = math.log2(math.e)
ln2 = math.log(2.0)
smallest = 1e-25
largest = 1e37
very_low = -3e38

f32 = jnp.float32
bf16 = jnp.bfloat16


def norms_of(points_ref, out_ref):
    for row in range(out_ref.shape[0]):
        part = points_ref[:, row * LANES : (row + 1) * LANES].astype(f32)
        out_ref[row : row + 1, :] = jnp.sum(part * part, axis=0, keepdims=True)


def transpose_points(points_ref, out_ref):
    dim, count = points_ref.shape
    for start in range(0, count, LANES):
        part = points_ref[:, start : start + LANES].astype(f32)
        part = jnp.concatenate([part, jnp.zeros((LANES - dim, LANES), f32)], axis=0)
        out_ref[start : start + LANES, :] = part.T.astype(bf16)


def to_columns(rows, out_ref):
    for row in range(rows.shape[0]):
        spread = jnp.broadcast_to(rows[row : row + 1, :], (LANES, LANES))
        out_ref[row * LANES : (row + 1) * LANES, :] = spread.T


def combine(parts):
    peak = jnp.max(parts, axis=0)
    return peak + jnp.log(jnp.sum(jnp.exp(parts - peak[None]), axis=0))


def in_range(total):
    return jnp.logical_and(jnp.min(total) >= smallest, jnp.max(total) <= largest)


class Static:
    def __init__(self, blocks, tiles):
        self.blocks, self.tiles = blocks, tiles

    def each(self, step):
        for b in range(self.blocks):
            for k in range(self.tiles):
                step(b, k, b, k)


class Listed:
    def __init__(self, list_ref, blocks, tiles):
        self.list_ref, self.blocks, self.tiles = list_ref, blocks, tiles
        self.room = (list_ref.shape[0] - 1) // 2

    def each(self, step):
        def group(index, carry):
            for u in range(UNROLL):
                at = index * UNROLL + u
                b = self.list_ref[at]
                k = self.list_ref[self.room + at]
                step(jnp.minimum(b, self.blocks - 1), jnp.minimum(k, self.tiles - 1), b, k)
            return carry

        lax.fori_loop(0, self.list_ref[2 * self.room], group, 0)


def at(index, size):
    if isinstance(index, int):
        return pl.ds(index * size, size)
    return pl.ds(pl.multiple_of(index * size, size), size)


def inner_of(right_ref, left_ref, b, k):
    dim = left_ref.shape[0]
    return jnp.dot(
        right_ref[at(k, TILE), :][:, :dim], left_ref[:, at(b, TILE)], preferred_element_type=f32
    )


def half(x, h):
    return x[:, h * LANES : (h + 1) * LANES]


def by_eights(x, op):
    return op(x.reshape(x.shape[0] // 8, 8, x.shape[1]), axis=0)


def row_of(ref, b, h):
    return ref[pl.ds(b * HALVES + h, 1), :]


def gather_columns(acc_ref, tiles, out_ref, op):
    for k in range(tiles):
        for h in range(HALVES):
            part = acc_ref[k, h * LANES : (h + 1) * LANES, :].T
            row = k * HALVES + h
            out_ref[row : row + 1, :] = op(part, axis=0, keepdims=True)


def gather_rows(acc_ref, blocks, out_ref, op):
    for b in range(blocks):
        part = op(acc_ref[b], axis=0, keepdims=True)
        for h in range(HALVES):
            row = b * HALVES + h
            out_ref[row : row + 1, :] = half(part, h)


def col_scores(weight, pot, left_norm, right_norm, right_ref, left_ref, pairs, scr, out_ref):
    dim = left_ref.shape[0]
    scale = 1.0 / (dim * eps)
    vec_ref, vec2_ref, _, _, acc_ref, col_ref, col2_ref = scr
    terms = weight + pot * (1.0 / eps)
    alpha = (terms - left_norm * (0.5 * scale)) * log2e
    top = jnp.max(alpha, keepdims=True)
    rows = alpha.shape[0]
    vec_ref[0:rows, :] = alpha - top
    acc_ref[...] = jnp.zeros(acc_ref.shape, f32)

    def add(b, k, to_b, to_k):
        z = inner_of(right_ref, left_ref, b, k) * (scale * log2e)
        parts = [jnp.exp2(half(z, h) + row_of(vec_ref, b, h)) for h in range(HALVES)]
        acc_ref[to_k] += functools.reduce(jnp.add, parts)

    pairs.each(add)
    gather_columns(acc_ref, pairs.tiles, out_ref, jnp.sum)
    total = out_ref[...]
    out_ref[...] = jnp.log(total) + top * ln2 - right_norm * (0.5 * scale)

    @pl.when(jnp.logical_not(in_range(total)))
    def _():
        vec_ref[0:rows, :] = terms
        vec2_ref[0:rows, :] = left_norm
        to_columns(right_norm, col_ref)
        acc_ref[...] = jnp.full(acc_ref.shape, very_low, f32)

        def scores(b, k):
            z = inner_of(right_ref, left_ref, b, k)
            tgt = col_ref[at(k, TILE), :]
            for h in range(HALVES):
                cost = (row_of(vec2_ref, b, h) + tgt - 2.0 * half(z, h)) * (1.0 / (2.0 * dim))
                yield row_of(vec_ref, b, h) - cost * (1.0 / eps)

        def highest(b, k, to_b, to_k):
            acc_ref[to_k] = functools.reduce(jnp.maximum, scores(b, k), acc_ref[to_k])

        pairs.each(highest)
        gather_columns(acc_ref, pairs.tiles, out_ref, jnp.max)
        peak = out_ref[...]
        to_columns(peak, col2_ref)
        acc_ref[...] = jnp.zeros(acc_ref.shape, f32)

        def add_exact(b, k, to_b, to_k):
            peaks = col2_ref[at(k, TILE), :]
            parts = [jnp.exp(s - peaks) for s in scores(b, k)]
            acc_ref[to_k] += functools.reduce(jnp.add, parts)

        pairs.each(add_exact)
        gather_columns(acc_ref, pairs.tiles, out_ref, jnp.sum)
        out_ref[...] = peak + jnp.log(out_ref[...])


def row_scores(weight, pot, right_norm, left_norm, right_ref, left_ref, pairs, scr, out_ref):
    dim = left_ref.shape[0]
    scale = 1.0 / (dim * eps)
    vec_ref, vec2_ref, acc_ref, _, _, col_ref, col2_ref = scr
    terms = weight + pot * (1.0 / eps)
    beta = (terms - right_norm * (0.5 * scale)) * log2e
    top = jnp.max(beta, keepdims=True)
    to_columns(beta - top, col_ref)
    acc_ref[...] = jnp.zeros(acc_ref.shape, f32)

    def add(b, k, to_b, to_k):
        z = inner_of(right_ref, left_ref, b, k) * (scale * log2e)
        tgt = col_ref[at(k, TILE), :]
        for h in range(HALVES):
            part = by_eights(jnp.exp2(half(z, h) + tgt), jnp.sum)
            acc_ref[to_b, :, h * LANES : (h + 1) * LANES] += part

    pairs.each(add)
    gather_rows(acc_ref, pairs.blocks, out_ref, jnp.sum)
    total = out_ref[...]
    out_ref[...] = jnp.log(total) + top * ln2 - left_norm * (0.5 * scale)

    @pl.when(jnp.logical_not(in_range(total)))
    def _():
        rows = left_norm.shape[0]
        to_columns(terms, col_ref)
        to_columns(right_norm, col2_ref)
        vec_ref[0:rows, :] = left_norm
        acc_ref[...] = jnp.full(acc_ref.shape, very_low, f32)

        def scores(b, k):
            z = inner_of(right_ref, left_ref, b, k)
            for h in range(HALVES):
                cost = (row_of(vec_ref, b, h) + col2_ref[at(k, TILE), :] - 2.0 * half(z, h)) * (
                    1.0 / (2.0 * dim)
                )
                yield col_ref[at(k, TILE), :] - cost * (1.0 / eps)

        def highest(b, k, to_b, to_k):
            for h, s in enumerate(scores(b, k)):
                where = slice(h * LANES, (h + 1) * LANES)
                acc_ref[to_b, :, where] = jnp.maximum(
                    acc_ref[to_b, :, where], by_eights(s, jnp.max)
                )

        pairs.each(highest)
        gather_rows(acc_ref, pairs.blocks, out_ref, jnp.max)
        peak = out_ref[...]
        vec2_ref[0:rows, :] = peak
        acc_ref[...] = jnp.zeros(acc_ref.shape, f32)

        def add_exact(b, k, to_b, to_k):
            for h, s in enumerate(scores(b, k)):
                where = slice(h * LANES, (h + 1) * LANES)
                acc_ref[to_b, :, where] += by_eights(
                    jnp.exp(s - row_of(vec2_ref, b, h)), jnp.sum
                )

        pairs.each(add_exact)
        gather_rows(acc_ref, pairs.blocks, out_ref, jnp.sum)
        out_ref[...] = peak + jnp.log(out_ref[...])


def look_up(table, which, out_ref):
    table = table.T
    high = table.astype(bf16)
    rest = table - high.astype(f32)
    middle = rest.astype(bf16)
    low = (rest - middle.astype(f32)).astype(bf16)
    stack = jnp.concatenate([high, middle, low], axis=0)
    place = lax.broadcasted_iota(jnp.int32, (LANES, LANES), 0)
    for row in range(which.shape[0]):
        index = which[row : row + 1, :]
        hot = jnp.where(place == lax.shift_right_logical(index, 7), 1.0, 0.0).astype(bf16)
        found = jnp.dot(stack, hot, preferred_element_type=f32)
        value = found[:LANES] + found[LANES : 2 * LANES] + found[2 * LANES :]
        value = jnp.where(place == jnp.bitwise_and(index, LANES - 1), value, 0.0)
        out_ref[row : row + 1, :] = jnp.sum(value, axis=0, keepdims=True)


def to_all(out_ref, value, start=0):
    out_ref[:, start : start + value.shape[0], :] = jnp.broadcast_to(
        value[None], (out_ref.shape[0],) + value.shape
    )


def coarse_start(left_ref, points_ref, weight_ref, send_ref, right_ref, ln_ref, rn_ref, *scr):
    norms_of(left_ref, ln_ref)
    norms_of(points_ref, rn_ref)
    transpose_points(points_ref, right_ref)
    *scr, out_ref = scr
    pairs = Static(left_ref.shape[1] // TILE, points_ref.shape[1] // TILE)
    weight = weight_ref[...]
    pot = jnp.zeros(weight.shape, f32)
    col_scores(weight, pot, ln_ref[...], rn_ref[...], right_ref, left_ref, pairs, scr, out_ref)
    to_all(send_ref, out_ref[...])


def coarse_rows(recv_ref, left_ref, right_ref, ln_ref, rn_ref, weight_ref, send_ref, tgt_ref, *scr):
    *scr, out_ref = scr
    tgt = (-0.5 * eps) * combine(recv_ref[...])
    tgt_ref[...] = tgt
    pairs = Static(left_ref.shape[1] // TILE, right_ref.shape[0] // TILE)
    for step, pot in enumerate((jnp.zeros(tgt.shape, f32), tgt)):
        row_scores(
            weight_ref[...], pot, rn_ref[...], ln_ref[...], right_ref, left_ref, pairs, scr, out_ref
        )
        to_all(send_ref, out_ref[...], step * out_ref.shape[0])


def coarse_cols(recv_ref, left_ref, right_ref, ln_ref, rn_ref, weight_ref, send_ref, *scr):
    *scr, out_ref = scr
    lse = combine(recv_ref[...])
    rows = lse.shape[0] // 2
    first = (-0.5 * eps) * lse[:rows]
    second = 0.5 * (first - eps * lse[rows:])
    to_all(send_ref, second)
    pairs = Static(left_ref.shape[1] // TILE, right_ref.shape[0] // TILE)
    col_scores(
        weight_ref[...], first, ln_ref[...], rn_ref[...], right_ref, left_ref, pairs, scr, out_ref
    )
    to_all(send_ref, out_ref[...], rows)


def coarse_end(recv_ref, tgt_ref, send_ref):
    count = tgt_ref.shape[0]
    rows = recv_ref.shape[1] - count
    lse = combine(recv_ref[:, rows:, :])
    to_all(send_ref, 0.5 * (tgt_ref[...] - eps * lse))


def prepare(left_ref, points_ref, support_ref, counts_ref, right_ref, ln_ref, rn_ref, list_ref):
    blocks = left_ref.shape[1] // TILE
    tiles = points_ref.shape[1] // TILE
    most = support_ref.shape[2]
    room = (list_ref.shape[0] - 1) // 2

    def one_block(b, found):
        count = counts_ref[b, 0]
        for m in range(most):
            list_ref[found] = b
            list_ref[room + found] = support_ref[b, 0, m]
            found = found + jnp.where(m < count, 1, 0)
        return found

    found = lax.fori_loop(0, blocks, one_block, 0)
    for u in range(UNROLL):
        list_ref[found + u] = blocks
        list_ref[room + found + u] = tiles
    list_ref[2 * room] = lax.div(found + UNROLL - 1, UNROLL)
    norms_of(left_ref, ln_ref)
    norms_of(points_ref, rn_ref)
    transpose_points(points_ref, right_ref)


def fine_cols_first(
    list_ref, recv_ref, which_ref, left_ref, right_ref, ln_ref, rn_ref, weight_ref, send_ref, src_ref, *scr
):
    *scr, table_ref, out_ref = scr
    shards = recv_ref.shape[0]
    rows = table_ref.shape[0] // shards
    for shard in range(shards):
        table_ref[shard * rows : (shard + 1) * rows, :] = recv_ref[shard, 0:rows, :]
    look_up(table_ref[...], which_ref[...], src_ref)
    pairs = Listed(list_ref, left_ref.shape[1] // TILE, right_ref.shape[0] // TILE)
    col_scores(
        weight_ref[...], src_ref[...], ln_ref[...], rn_ref[...], right_ref, left_ref, pairs, scr, out_ref
    )
    to_all(send_ref, out_ref[...])


def fine_rows_first(
    list_ref, recv_ref, which_ref, left_ref, right_ref, ln_ref, rn_ref, weight_ref, out_ref, tgt_ref, *scr
):
    *scr, table_ref = scr
    shards = recv_ref.shape[0]
    rows = table_ref.shape[0] // shards
    for shard in range(shards):
        table_ref[shard * rows : (shard + 1) * rows, :] = recv_ref[shard]
    look_up(table_ref[...], which_ref[...], tgt_ref)
    pairs = Listed(list_ref, left_ref.shape[1] // TILE, right_ref.shape[0] // TILE)
    row_scores(
        weight_ref[...], tgt_ref[...], rn_ref[...], ln_ref[...], right_ref, left_ref, pairs, scr, out_ref
    )


def fine_rows_second(
    list_ref, recv_ref, tgt_ref, first_ref, left_ref, right_ref, ln_ref, rn_ref, weight_ref, send_ref, new_ref, *scr
):
    *scr, out_ref = scr
    new_ref[...] = 0.5 * (tgt_ref[...] - eps * combine(recv_ref[...]))
    pairs = Listed(list_ref, left_ref.shape[1] // TILE, right_ref.shape[0] // TILE)
    row_scores(
        weight_ref[...], new_ref[...], rn_ref[...], ln_ref[...], right_ref, left_ref, pairs, scr, out_ref
    )
    shards, rows, _ = send_ref.shape
    rows = rows // 2
    for shard in range(shards):
        where = slice(shard * rows, (shard + 1) * rows)
        send_ref[shard, 0:rows, :] = first_ref[where, :]
        send_ref[shard, rows : 2 * rows, :] = out_ref[where, :]


def combine_rows(recv_ref, send_ref):
    to_all(send_ref, combine(recv_ref[...]))


def fine_cols_second(
    list_ref, recv_ref, src_ref, left_ref, right_ref, ln_ref, rn_ref, weight_ref, send_ref, new_ref, *scr
):
    *scr, first_ref, out_ref = scr
    shards, rows, _ = recv_ref.shape
    rows = rows // 2
    for shard in range(shards):
        where = slice(shard * rows, (shard + 1) * rows)
        first = 0.5 * (src_ref[where, :] - eps * recv_ref[shard, 0:rows, :])
        first_ref[where, :] = first
        new_ref[where, :] = 0.5 * (first - eps * recv_ref[shard, rows : 2 * rows, :])
    pairs = Listed(list_ref, left_ref.shape[1] // TILE, right_ref.shape[0] // TILE)
    col_scores(
        weight_ref[...], first_ref[...], ln_ref[...], rn_ref[...], right_ref, left_ref, pairs, scr, out_ref
    )
    to_all(send_ref, out_ref[...])


def fine_end(recv_ref, tgt_ref, out_ref):
    out_ref[...] = 0.5 * (tgt_ref[...] - eps * combine(recv_ref[...]))


def scratch_for(left, right, spare):
    rows = left // LANES
    return [
        pltpu.VMEM((rows, LANES), f32),
        pltpu.VMEM((rows, LANES), f32),
        pltpu.VMEM((left // TILE + spare, 8, TILE), f32),
        pltpu.VMEM((8, LANES), f32),
        pltpu.VMEM((right // TILE + spare, TILE, LANES), f32),
        pltpu.VMEM((right, LANES), f32),
        pltpu.VMEM((right, LANES), f32),
    ]


def call(body, outs, operands, scratch=(), smem=(), smem_out=(), work=0):
    spaces = [pltpu.SMEM if i in smem else pltpu.VMEM for i in range(len(operands))]
    out_spaces = [pltpu.SMEM if i in smem_out else pltpu.VMEM for i in range(len(outs))]
    return pl.pallas_call(
        body,
        out_shape=[jax.ShapeDtypeStruct(shape, dtype) for shape, dtype in outs],
        in_specs=[pl.BlockSpec(memory_space=s) for s in spaces],
        out_specs=[pl.BlockSpec(memory_space=s) for s in out_spaces],
        scratch_shapes=list(scratch),
        compiler_params=pltpu.CompilerParams(vmem_limit_bytes=24 * 1024 * 1024),
        cost_estimate=pl.CostEstimate(
            flops=128 * work + 1000, bytes_accessed=1 << 20, transcendentals=work
        ),
    )(*operands)


def exchange(x, axis):
    return lax.all_to_all(x, axis, 0, 0, tiled=True)


def per_device(
    n_src,
    n_tgt,
    src_centroids,
    tgt_centroids,
    src_weights,
    tgt_weights,
    src_cells,
    tgt_cells,
    src_mass,
    tgt_mass,
    src_cluster,
    tgt_cluster,
    support,
    counts,
):
    cs, ct = src_centroids.shape[1], tgt_centroids.shape[1]
    fs, ft = src_cells.shape[1], tgt_cells.shape[1]
    csr, ctr, fsr, ftr = (n // LANES for n in (cs, ct, fs, ft))
    vec = lambda x: x.reshape(-1, LANES)
    src_weights, tgt_weights, src_mass, tgt_mass, src_cluster, tgt_cluster = map(
        vec, (src_weights, tgt_weights, src_mass, tgt_mass, src_cluster, tgt_cluster)
    )
    coarse_scratch = scratch_for(cs, ct, 0)
    fine_scratch = scratch_for(fs, ft, 1)
    one = lambda rows: pltpu.VMEM((rows, LANES), f32)
    coarse_work = cs * ct
    fine_work = fs * ft // 4

    send, right, ln, rn = call(
        coarse_start,
        [((n_src, ctr, LANES), f32), ((ct, LANES), bf16), ((csr, LANES), f32), ((ctr, LANES), f32)],
        [src_centroids, tgt_centroids, src_weights],
        coarse_scratch + [one(ctr)],
        work=coarse_work,
    )
    recv = exchange(send, "src")
    room = support.shape[0] * support.shape[2] + UNROLL
    fine_right, fine_ln, fine_rn, listed = call(
        prepare,
        [
            ((ft, LANES), bf16),
            ((fsr, LANES), f32),
            ((ftr, LANES), f32),
            ((2 * room + 1,), jnp.int32),
        ],
        [src_cells, tgt_cells, support, counts],
        smem=(2, 3),
        smem_out=(3,),
        work=coarse_work,
    )
    send, coarse_tgt = call(
        coarse_rows,
        [((n_tgt, 2 * csr, LANES), f32), ((ctr, LANES), f32)],
        [recv, src_centroids, right, ln, rn, tgt_weights],
        coarse_scratch + [one(csr)],
        work=2 * coarse_work,
    )
    recv = exchange(send, "tgt")
    (send,) = call(
        coarse_cols,
        [((n_src, csr + ctr, LANES), f32)],
        [recv, src_centroids, right, ln, rn, src_weights],
        coarse_scratch + [one(ctr)],
        work=coarse_work,
    )
    every_src = exchange(send, "src")
    (send,) = call(coarse_end, [((n_tgt, ctr, LANES), f32)], [every_src, coarse_tgt])
    every_tgt = exchange(send, "tgt")

    fine_static = [src_cells, fine_right, fine_ln, fine_rn]
    send, fine_src = call(
        fine_cols_first,
        [((n_src, ftr, LANES), f32), ((fsr, LANES), f32)],
        [listed, every_src, src_cluster, *fine_static, src_mass],
        fine_scratch + [one(n_src * csr), one(ftr)],
        smem=(0,),
        work=fine_work,
    )
    recv = exchange(send, "src")
    first_rows, fine_tgt = call(
        fine_rows_first,
        [((fsr, LANES), f32), ((ftr, LANES), f32)],
        [listed, every_tgt, tgt_cluster, *fine_static, tgt_mass],
        fine_scratch + [one(n_tgt * ctr)],
        smem=(0,),
        work=fine_work,
    )
    send, fine_tgt = call(
        fine_rows_second,
        [((n_tgt, 2 * fsr // n_tgt, LANES), f32), ((ftr, LANES), f32)],
        [listed, recv, fine_tgt, first_rows, *fine_static, tgt_mass],
        fine_scratch + [one(fsr)],
        smem=(0,),
        work=fine_work,
    )
    recv = exchange(send, "tgt")
    (send,) = call(combine_rows, [(recv.shape, f32)], [recv])
    recv = exchange(send, "tgt")
    send, fine_src = call(
        fine_cols_second,
        [((n_src, ftr, LANES), f32), ((fsr, LANES), f32)],
        [listed, recv, fine_src, *fine_static, src_mass],
        fine_scratch + [one(fsr), one(ftr)],
        smem=(0,),
        work=fine_work,
    )
    recv = exchange(send, "src")
    (fine_tgt,) = call(fine_end, [((ftr, LANES), f32)], [recv, fine_tgt])
    return (fine_src.reshape(fs), fine_tgt.reshape(ft))


def solution(mesh):
    in_specs = (
        P(None, "src"),
        P(None, "tgt"),
        P("src"),
        P("tgt"),
        P(None, "src"),
        P(None, "tgt"),
        P("src"),
        P("tgt"),
        P("src"),
        P("tgt"),
        P("src", "tgt", None),
        P("src", "tgt"),
    )
    out_specs = (P("src"), P("tgt"))
    body = functools.partial(per_device, mesh.shape["src"], mesh.shape["tgt"])
    return jax.shard_map(body, mesh=mesh, in_specs=in_specs, out_specs=out_specs, check_vma=False)
```

```python
import functools
import math
import jax
import jax.numpy as jnp
from jax import lax
from jax.experimental import pallas as pl
from jax.experimental.pallas import tpu as pltpu
from jax.sharding import PartitionSpec as P

TILE = 256
LANES = 128
HALVES = TILE // LANES
UNROLL = 16

eps = 0.0625
log2e = math.log2(math.e)
ln2 = math.log(2.0)
smallest = 1e-25
largest = 1e37
very_low = -3e38

f32 = jnp.float32
bf16 = jnp.bfloat16


def norms_of(points_ref, out_ref):
    for row in range(out_ref.shape[0]):
        part = points_ref[:, row * LANES : (row + 1) * LANES].astype(f32)
        out_ref[row : row + 1, :] = jnp.sum(part * part, axis=0, keepdims=True)


def transpose_points(points_ref, out_ref):
    dim, count = points_ref.shape
    for start in range(0, count, LANES):
        part = points_ref[:, start : start + LANES].astype(f32)
        part = jnp.concatenate([part, jnp.zeros((LANES - dim, LANES), f32)], axis=0)
        out_ref[start : start + LANES, :] = part.T.astype(bf16)


def to_columns(rows, out_ref):
    for row in range(rows.shape[0]):
        spread = jnp.broadcast_to(rows[row : row + 1, :], (LANES, LANES))
        out_ref[row * LANES : (row + 1) * LANES, :] = spread.T


def prepare_points(left_ref, points_ref, right_ref, ln_ref, rn_ref):
    norms_of(left_ref, ln_ref)
    norms_of(points_ref, rn_ref)
    transpose_points(points_ref, right_ref)


def combine(parts):
    peak = jnp.max(parts, axis=0)
    return peak + jnp.log(jnp.sum(jnp.exp(parts - peak[None]), axis=0))


def in_range(total):
    return jnp.logical_and(jnp.min(total) >= smallest, jnp.max(total) <= largest)


class Static:
    def __init__(self, blocks, tiles):
        self.blocks, self.tiles = blocks, tiles

    def each(self, step):
        for b in range(self.blocks):
            for k in range(self.tiles):
                step(b, k, b, k)


class Listed:
    def __init__(self, list_ref, blocks, tiles):
        self.list_ref, self.blocks, self.tiles = list_ref, blocks, tiles
        self.room = (list_ref.shape[0] - 1) // 2

    def each(self, step):
        def group(index, carry):
            for u in range(UNROLL):
                at = index * UNROLL + u
                b = self.list_ref[at]
                k = self.list_ref[self.room + at]
                step(jnp.minimum(b, self.blocks - 1), jnp.minimum(k, self.tiles - 1), b, k)
            return carry

        lax.fori_loop(0, self.list_ref[2 * self.room], group, 0)


def at(index, size):
    if isinstance(index, int):
        return pl.ds(index * size, size)
    return pl.ds(pl.multiple_of(index * size, size), size)


def inner_of(right_ref, left_ref, b, k):
    dim = left_ref.shape[0]
    return jnp.dot(
        right_ref[at(k, TILE), :][:, :dim], left_ref[:, at(b, TILE)], preferred_element_type=f32
    )


def half(x, h):
    return x[:, h * LANES : (h + 1) * LANES]


def by_eights(x, op):
    return op(x.reshape(x.shape[0] // 8, 8, x.shape[1]), axis=0)


def row_of(ref, b, h):
    return ref[pl.ds(b * HALVES + h, 1), :]


def gather_columns(acc_ref, tiles, out_ref, op):
    for k in range(tiles):
        for h in range(HALVES):
            part = acc_ref[k, h * LANES : (h + 1) * LANES, :].T
            row = k * HALVES + h
            out_ref[row : row + 1, :] = op(part, axis=0, keepdims=True)


def gather_rows(acc_ref, blocks, out_ref, op):
    for b in range(blocks):
        part = op(acc_ref[b], axis=0, keepdims=True)
        for h in range(HALVES):
            row = b * HALVES + h
            out_ref[row : row + 1, :] = half(part, h)


def col_scores(weight, pot, left_norm, right_norm, right_ref, left_ref, pairs, scr, out_ref):
    dim = left_ref.shape[0]
    scale = 1.0 / (dim * eps)
    vec_ref, vec2_ref, _, _, acc_ref, col_ref, col2_ref = scr
    terms = weight + pot * (1.0 / eps)
    alpha = (terms - left_norm * (0.5 * scale)) * log2e
    top = jnp.max(alpha, keepdims=True)
    rows = alpha.shape[0]
    vec_ref[0:rows, :] = alpha - top
    acc_ref[...] = jnp.zeros(acc_ref.shape, f32)

    def add(b, k, to_b, to_k):
        z = inner_of(right_ref, left_ref, b, k) * (scale * log2e)
        parts = [jnp.exp2(half(z, h) + row_of(vec_ref, b, h)) for h in range(HALVES)]
        acc_ref[to_k] += functools.reduce(jnp.add, parts)

    pairs.each(add)
    gather_columns(acc_ref, pairs.tiles, out_ref, jnp.sum)
    total = out_ref[...]
    out_ref[...] = jnp.log(total) + top * ln2 - right_norm * (0.5 * scale)

    @pl.when(jnp.logical_not(in_range(total)))
    def _():
        vec_ref[0:rows, :] = terms
        vec2_ref[0:rows, :] = left_norm
        to_columns(right_norm, col_ref)
        acc_ref[...] = jnp.full(acc_ref.shape, very_low, f32)

        def scores(b, k):
            z = inner_of(right_ref, left_ref, b, k)
            tgt = col_ref[at(k, TILE), :]
            for h in range(HALVES):
                cost = (row_of(vec2_ref, b, h) + tgt - 2.0 * half(z, h)) * (1.0 / (2.0 * dim))
                yield row_of(vec_ref, b, h) - cost * (1.0 / eps)

        def highest(b, k, to_b, to_k):
            acc_ref[to_k] = functools.reduce(jnp.maximum, scores(b, k), acc_ref[to_k])

        pairs.each(highest)
        gather_columns(acc_ref, pairs.tiles, out_ref, jnp.max)
        peak = out_ref[...]
        to_columns(peak, col2_ref)
        acc_ref[...] = jnp.zeros(acc_ref.shape, f32)

        def add_exact(b, k, to_b, to_k):
            peaks = col2_ref[at(k, TILE), :]
            parts = [jnp.exp(s - peaks) for s in scores(b, k)]
            acc_ref[to_k] += functools.reduce(jnp.add, parts)

        pairs.each(add_exact)
        gather_columns(acc_ref, pairs.tiles, out_ref, jnp.sum)
        out_ref[...] = peak + jnp.log(out_ref[...])


def row_scores(weight, pot, right_norm, left_norm, right_ref, left_ref, pairs, scr, out_ref):
    dim = left_ref.shape[0]
    scale = 1.0 / (dim * eps)
    vec_ref, vec2_ref, acc_ref, _, _, col_ref, col2_ref = scr
    terms = weight + pot * (1.0 / eps)
    beta = (terms - right_norm * (0.5 * scale)) * log2e
    top = jnp.max(beta, keepdims=True)
    to_columns(beta - top, col_ref)
    acc_ref[...] = jnp.zeros(acc_ref.shape, f32)

    def add(b, k, to_b, to_k):
        z = inner_of(right_ref, left_ref, b, k) * (scale * log2e)
        tgt = col_ref[at(k, TILE), :]
        for h in range(HALVES):
            part = by_eights(jnp.exp2(half(z, h) + tgt), jnp.sum)
            acc_ref[to_b, :, h * LANES : (h + 1) * LANES] += part

    pairs.each(add)
    gather_rows(acc_ref, pairs.blocks, out_ref, jnp.sum)
    total = out_ref[...]
    out_ref[...] = jnp.log(total) + top * ln2 - left_norm * (0.5 * scale)

    @pl.when(jnp.logical_not(in_range(total)))
    def _():
        rows = left_norm.shape[0]
        to_columns(terms, col_ref)
        to_columns(right_norm, col2_ref)
        vec_ref[0:rows, :] = left_norm
        acc_ref[...] = jnp.full(acc_ref.shape, very_low, f32)

        def scores(b, k):
            z = inner_of(right_ref, left_ref, b, k)
            for h in range(HALVES):
                cost = (row_of(vec_ref, b, h) + col2_ref[at(k, TILE), :] - 2.0 * half(z, h)) * (
                    1.0 / (2.0 * dim)
                )
                yield col_ref[at(k, TILE), :] - cost * (1.0 / eps)

        def highest(b, k, to_b, to_k):
            for h, s in enumerate(scores(b, k)):
                where = slice(h * LANES, (h + 1) * LANES)
                acc_ref[to_b, :, where] = jnp.maximum(
                    acc_ref[to_b, :, where], by_eights(s, jnp.max)
                )

        pairs.each(highest)
        gather_rows(acc_ref, pairs.blocks, out_ref, jnp.max)
        peak = out_ref[...]
        vec2_ref[0:rows, :] = peak
        acc_ref[...] = jnp.zeros(acc_ref.shape, f32)

        def add_exact(b, k, to_b, to_k):
            for h, s in enumerate(scores(b, k)):
                where = slice(h * LANES, (h + 1) * LANES)
                acc_ref[to_b, :, where] += by_eights(
                    jnp.exp(s - row_of(vec2_ref, b, h)), jnp.sum
                )

        pairs.each(add_exact)
        gather_rows(acc_ref, pairs.blocks, out_ref, jnp.sum)
        out_ref[...] = peak + jnp.log(out_ref[...])


def look_up(table, which, out_ref):
    table = table.T
    high = table.astype(bf16)
    rest = table - high.astype(f32)
    middle = rest.astype(bf16)
    low = (rest - middle.astype(f32)).astype(bf16)
    upper = jnp.concatenate([high, middle], axis=1)
    place = lax.broadcasted_iota(jnp.int32, (LANES, TILE), 0)
    for row in range(0, which.shape[0], HALVES):
        index = jnp.concatenate([which[row + h : row + h + 1, :] for h in range(HALVES)], axis=1)
        hot = jnp.where(place == lax.shift_right_logical(index, 7), 1.0, 0.0).astype(bf16)
        value = jnp.dot(upper, jnp.concatenate([hot, hot], axis=0), preferred_element_type=f32)
        value = value + jnp.dot(low, hot, preferred_element_type=f32)
        value = jnp.where(place == jnp.bitwise_and(index, LANES - 1), value, 0.0)
        value = jnp.sum(value, axis=0, keepdims=True)
        for h in range(HALVES):
            out_ref[row + h : row + h + 1, :] = half(value, h)


def to_all(out_ref, value, start=0):
    out_ref[:, start : start + value.shape[0], :] = jnp.broadcast_to(
        value[None], (out_ref.shape[0],) + value.shape
    )


def coarse_start(src_ref, tgt_ref, from_ref, send_ref, *scr):
    *scr, out_ref, left_ref, points_ref, weight_ref, right_ref, ln_ref, rn_ref, sems = scr
    moves = ((src_ref, left_ref), (tgt_ref, points_ref), (from_ref, weight_ref))
    copies = [pltpu.make_async_copy(a, b, sems.at[i]) for i, (a, b) in enumerate(moves)]
    for copy in copies:
        copy.start()
    for copy in copies:
        copy.wait()
    prepare_points(left_ref, points_ref, right_ref, ln_ref, rn_ref)
    pairs = Static(left_ref.shape[1] // TILE, points_ref.shape[1] // TILE)
    weight = weight_ref[...]
    pot = jnp.zeros(weight.shape, f32)
    col_scores(weight, pot, ln_ref[...], rn_ref[...], right_ref, left_ref, pairs, scr, out_ref)
    to_all(send_ref, out_ref[...])


def coarse_rows(recv_ref, left_ref, right_ref, ln_ref, rn_ref, weight_ref, send_ref, tgt_ref, *scr):
    *scr, out_ref = scr
    tgt = (-0.5 * eps) * combine(recv_ref[...])
    tgt_ref[...] = tgt
    pairs = Static(left_ref.shape[1] // TILE, right_ref.shape[0] // TILE)
    for step, pot in enumerate((jnp.zeros(tgt.shape, f32), tgt)):
        row_scores(
            weight_ref[...], pot, rn_ref[...], ln_ref[...], right_ref, left_ref, pairs, scr, out_ref
        )
        to_all(send_ref, out_ref[...], step * out_ref.shape[0])


def coarse_cols(
    recv_ref, left_ref, right_ref, ln_ref, rn_ref, weight_ref, after_ref, send_ref, *scr
):
    *scr, out_ref = scr
    lse = combine(recv_ref[...])
    rows = lse.shape[0] // 2
    first = (-0.5 * eps) * lse[:rows]
    second = 0.5 * (first - eps * lse[rows:])
    to_all(send_ref, second)
    pairs = Static(left_ref.shape[1] // TILE, right_ref.shape[0] // TILE)
    col_scores(
        weight_ref[...], first, ln_ref[...], rn_ref[...], right_ref, left_ref, pairs, scr, out_ref
    )
    to_all(send_ref, out_ref[...], rows)


def coarse_end(recv_ref, tgt_ref, send_ref):
    count = tgt_ref.shape[0]
    rows = recv_ref.shape[1] - count
    lse = combine(recv_ref[:, rows:, :])
    to_all(send_ref, 0.5 * (tgt_ref[...] - eps * lse))


def prepare(
    left_ref, points_ref, support_ref, counts_ref, after_ref, right_ref, ln_ref, rn_ref, list_ref
):
    blocks = left_ref.shape[1] // TILE
    tiles = points_ref.shape[1] // TILE
    most = support_ref.shape[2]
    room = (list_ref.shape[0] - 1) // 2

    def one_block(b, found):
        count = counts_ref[b, 0]
        for m in range(most):
            list_ref[found] = b
            list_ref[room + found] = support_ref[b, 0, m]
            found = found + jnp.where(m < count, 1, 0)
        return found

    found = lax.fori_loop(0, blocks, one_block, 0)
    for u in range(UNROLL):
        list_ref[found + u] = blocks
        list_ref[room + found + u] = tiles
    list_ref[2 * room] = lax.div(found + UNROLL - 1, UNROLL)
    prepare_points(left_ref, points_ref, right_ref, ln_ref, rn_ref)


def fine_cols_first(
    list_ref, recv_ref, which_ref, left_ref, right_ref, ln_ref, rn_ref, weight_ref, send_ref, src_ref, *scr
):
    *scr, table_ref, out_ref = scr
    shards = recv_ref.shape[0]
    rows = table_ref.shape[0] // shards
    for shard in range(shards):
        table_ref[shard * rows : (shard + 1) * rows, :] = recv_ref[shard, 0:rows, :]
    look_up(table_ref[...], which_ref[...], src_ref)
    pairs = Listed(list_ref, left_ref.shape[1] // TILE, right_ref.shape[0] // TILE)
    col_scores(
        weight_ref[...], src_ref[...], ln_ref[...], rn_ref[...], right_ref, left_ref, pairs, scr, out_ref
    )
    to_all(send_ref, out_ref[...])


def fine_rows_first(
    list_ref, recv_ref, which_ref, left_ref, right_ref, ln_ref, rn_ref, weight_ref, out_ref, tgt_ref, *scr
):
    *scr, table_ref = scr
    shards = recv_ref.shape[0]
    rows = table_ref.shape[0] // shards
    for shard in range(shards):
        table_ref[shard * rows : (shard + 1) * rows, :] = recv_ref[shard]
    look_up(table_ref[...], which_ref[...], tgt_ref)
    pairs = Listed(list_ref, left_ref.shape[1] // TILE, right_ref.shape[0] // TILE)
    row_scores(
        weight_ref[...], tgt_ref[...], rn_ref[...], ln_ref[...], right_ref, left_ref, pairs, scr, out_ref
    )


def fine_rows_second(
    list_ref, recv_ref, tgt_ref, first_ref, left_ref, right_ref, ln_ref, rn_ref, weight_ref, send_ref, new_ref, *scr
):
    *scr, out_ref = scr
    new_ref[...] = 0.5 * (tgt_ref[...] - eps * combine(recv_ref[...]))
    pairs = Listed(list_ref, left_ref.shape[1] // TILE, right_ref.shape[0] // TILE)
    row_scores(
        weight_ref[...], new_ref[...], rn_ref[...], ln_ref[...], right_ref, left_ref, pairs, scr, out_ref
    )
    shards, rows, _ = send_ref.shape
    rows = rows // 2
    for shard in range(shards):
        where = slice(shard * rows, (shard + 1) * rows)
        send_ref[shard, 0:rows, :] = first_ref[where, :]
        send_ref[shard, rows : 2 * rows, :] = out_ref[where, :]


def combine_rows(recv_ref, send_ref):
    to_all(send_ref, combine(recv_ref[...]))


def fine_cols_second(
    list_ref, recv_ref, src_ref, left_ref, right_ref, ln_ref, rn_ref, weight_ref, send_ref, new_ref, *scr
):
    *scr, first_ref, out_ref = scr
    shards, rows, _ = recv_ref.shape
    rows = rows // 2
    for shard in range(shards):
        where = slice(shard * rows, (shard + 1) * rows)
        first = 0.5 * (src_ref[where, :] - eps * recv_ref[shard, 0:rows, :])
        first_ref[where, :] = first
        new_ref[where, :] = 0.5 * (first - eps * recv_ref[shard, rows : 2 * rows, :])
    pairs = Listed(list_ref, left_ref.shape[1] // TILE, right_ref.shape[0] // TILE)
    col_scores(
        weight_ref[...], first_ref[...], ln_ref[...], rn_ref[...], right_ref, left_ref, pairs, scr, out_ref
    )
    to_all(send_ref, out_ref[...])


def fine_end(recv_ref, tgt_ref, out_ref):
    out_ref[...] = 0.5 * (tgt_ref[...] - eps * combine(recv_ref[...]))


def scratch_for(left, right, spare):
    rows = left // LANES
    return [
        pltpu.VMEM((rows, LANES), f32),
        pltpu.VMEM((rows, LANES), f32),
        pltpu.VMEM((left // TILE + spare, 8, TILE), f32),
        pltpu.VMEM((8, LANES), f32),
        pltpu.VMEM((right // TILE + spare, TILE, LANES), f32),
        pltpu.VMEM((right, LANES), f32),
        pltpu.VMEM((right, LANES), f32),
    ]


def call(body, outs, operands, scratch=(), smem=(), smem_out=(), hbm=(), work=0, limit=24):
    spaces = [
        pltpu.SMEM if i in smem else pltpu.HBM if i in hbm else pltpu.VMEM for i in range(len(operands))
    ]
    out_spaces = [pltpu.SMEM if i in smem_out else pltpu.VMEM for i in range(len(outs))]
    return pl.pallas_call(
        body,
        out_shape=[jax.ShapeDtypeStruct(shape, dtype) for shape, dtype in outs],
        in_specs=[pl.BlockSpec(memory_space=s) for s in spaces],
        out_specs=[pl.BlockSpec(memory_space=s) for s in out_spaces],
        scratch_shapes=list(scratch),
        compiler_params=pltpu.CompilerParams(vmem_limit_bytes=limit * 1024 * 1024),
        cost_estimate=pl.CostEstimate(
            flops=128 * work + 1000, bytes_accessed=1 << 20, transcendentals=work
        ),
    )(*operands)


def exchange(x, axis):
    return lax.all_to_all(x, axis, 0, 0, tiled=True)


def per_device(
    n_src,
    n_tgt,
    src_centroids,
    tgt_centroids,
    src_weights,
    tgt_weights,
    src_cells,
    tgt_cells,
    src_mass,
    tgt_mass,
    src_cluster,
    tgt_cluster,
    support,
    counts,
):
    cs, ct = src_centroids.shape[1], tgt_centroids.shape[1]
    fs, ft = src_cells.shape[1], tgt_cells.shape[1]
    csr, ctr, fsr, ftr = (n // LANES for n in (cs, ct, fs, ft))
    vec = lambda x: x.reshape(-1, LANES)
    src_weights, tgt_weights, src_mass, tgt_mass, src_cluster, tgt_cluster = map(
        vec, (src_weights, tgt_weights, src_mass, tgt_mass, src_cluster, tgt_cluster)
    )
    coarse_scratch = scratch_for(cs, ct, 0)
    fine_scratch = scratch_for(fs, ft, 1)
    one = lambda rows: pltpu.VMEM((rows, LANES), f32)
    coarse_work = cs * ct
    fine_work = fs * ft // 4

    (send,) = call(
        coarse_start,
        [((n_src, ctr, LANES), f32)],
        [src_centroids, tgt_centroids, src_weights],
        coarse_scratch
        + [
            one(ctr),
            pltpu.VMEM(src_centroids.shape, bf16),
            pltpu.VMEM(tgt_centroids.shape, bf16),
            one(csr),
            pltpu.VMEM((ct, LANES), bf16),
            one(csr),
            one(ctr),
            pltpu.SemaphoreType.DMA((3,)),
        ],
        hbm=(0, 1, 2),
        limit=64,
        work=coarse_work,
    )
    recv = exchange(send, "src")
    right, ln, rn = call(
        prepare_points,
        [((ct, LANES), bf16), ((csr, LANES), f32), ((ctr, LANES), f32)],
        [src_centroids, tgt_centroids],
        work=coarse_work,
    )
    send, coarse_tgt = call(
        coarse_rows,
        [((n_tgt, 2 * csr, LANES), f32), ((ctr, LANES), f32)],
        [recv, src_centroids, right, ln, rn, tgt_weights],
        coarse_scratch + [one(csr)],
        work=2 * coarse_work,
    )
    room = support.shape[0] * support.shape[2] + UNROLL
    fine_right, fine_ln, fine_rn, listed = call(
        prepare,
        [
            ((ft, LANES), bf16),
            ((fsr, LANES), f32),
            ((ftr, LANES), f32),
            ((2 * room + 1,), jnp.int32),
        ],
        [src_cells, tgt_cells, support, counts, coarse_tgt],
        smem=(2, 3),
        smem_out=(3,),
        work=2 * coarse_work,
    )
    recv = exchange(send, "tgt")
    (send,) = call(
        coarse_cols,
        [((n_src, csr + ctr, LANES), f32)],
        [recv, src_centroids, right, ln, rn, src_weights, fine_rn],
        coarse_scratch + [one(ctr)],
        work=coarse_work,
    )
    every_src = exchange(send, "src")
    (send,) = call(coarse_end, [((n_tgt, ctr, LANES), f32)], [every_src, coarse_tgt])
    every_tgt = exchange(send, "tgt")

    fine_static = [src_cells, fine_right, fine_ln, fine_rn]
    send, fine_src = call(
        fine_cols_first,
        [((n_src, ftr, LANES), f32), ((fsr, LANES), f32)],
        [listed, every_src, src_cluster, *fine_static, src_mass],
        fine_scratch + [one(n_src * csr), one(ftr)],
        smem=(0,),
        work=fine_work,
    )
    recv = exchange(send, "src")
    first_rows, fine_tgt = call(
        fine_rows_first,
        [((fsr, LANES), f32), ((ftr, LANES), f32)],
        [listed, every_tgt, tgt_cluster, *fine_static, tgt_mass],
        fine_scratch + [one(n_tgt * ctr)],
        smem=(0,),
        work=fine_work,
    )
    send, fine_tgt = call(
        fine_rows_second,
        [((n_tgt, 2 * fsr // n_tgt, LANES), f32), ((ftr, LANES), f32)],
        [listed, recv, fine_tgt, first_rows, *fine_static, tgt_mass],
        fine_scratch + [one(fsr)],
        smem=(0,),
        work=fine_work,
    )
    recv = exchange(send, "tgt")
    (send,) = call(combine_rows, [(recv.shape, f32)], [recv])
    recv = exchange(send, "tgt")
    send, fine_src = call(
        fine_cols_second,
        [((n_src, ftr, LANES), f32), ((fsr, LANES), f32)],
        [listed, recv, fine_src, *fine_static, src_mass],
        fine_scratch + [one(fsr), one(ftr)],
        smem=(0,),
        work=fine_work,
    )
    recv = exchange(send, "src")
    (fine_tgt,) = call(fine_end, [((ftr, LANES), f32)], [recv, fine_tgt])
    return (fine_src.reshape(fs), fine_tgt.reshape(ft))


def solution(mesh):
    in_specs = (
        P(None, "src"),
        P(None, "tgt"),
        P("src"),
        P("tgt"),
        P(None, "src"),
        P(None, "tgt"),
        P("src"),
        P("tgt"),
        P("src"),
        P("tgt"),
        P("src", "tgt", None),
        P("src", "tgt"),
    )
    out_specs = (P("src"), P("tgt"))
    body = functools.partial(per_device, mesh.shape["src"], mesh.shape["tgt"])
    return jax.shard_map(body, mesh=mesh, in_specs=in_specs, out_specs=out_specs, check_vma=False)
```

```python
import functools
import math
import jax
import jax.numpy as jnp
from jax import lax
from jax.experimental import pallas as pl
from jax.experimental.pallas import tpu as pltpu
from jax.sharding import PartitionSpec as P

TILE = 256
LANES = 128
HALVES = TILE // LANES
UNROLL = 32
TAIL = 16

eps = 0.0625
log2e = math.log2(math.e)
ln2 = math.log(2.0)
smallest = 1e-25
largest = 1e37
very_low = -3e38

f32 = jnp.float32
bf16 = jnp.bfloat16


def norms_of(points_ref, out_ref):
    for row in range(out_ref.shape[0]):
        part = points_ref[:, row * LANES : (row + 1) * LANES].astype(f32)
        out_ref[row : row + 1, :] = jnp.sum(part * part, axis=0, keepdims=True)


def transpose_points(points_ref, out_ref):
    dim, count = points_ref.shape
    for start in range(0, count, LANES):
        part = points_ref[:, start : start + LANES].astype(f32)
        part = jnp.concatenate([part, jnp.zeros((LANES - dim, LANES), f32)], axis=0)
        out_ref[start : start + LANES, :] = part.T.astype(bf16)


def to_columns(rows, out_ref):
    for row in range(rows.shape[0]):
        spread = jnp.broadcast_to(rows[row : row + 1, :], (LANES, LANES))
        out_ref[row * LANES : (row + 1) * LANES, :] = spread.T


def prepare_points(left_ref, points_ref, right_ref, ln_ref, rn_ref):
    norms_of(left_ref, ln_ref)
    norms_of(points_ref, rn_ref)
    transpose_points(points_ref, right_ref)


def combine(parts):
    peak = jnp.max(parts, axis=0)
    return peak + jnp.log(jnp.sum(jnp.exp(parts - peak[None]), axis=0))


def in_range(total):
    return jnp.logical_and(jnp.min(total) >= smallest, jnp.max(total) <= largest)


class Static:
    def __init__(self, blocks, tiles):
        self.blocks, self.tiles = blocks, tiles

    def each(self, step, unroll=1, tail=1):
        for b in range(self.blocks):
            for k in range(self.tiles):
                step(b, k, b, k)


class Listed:
    def __init__(self, list_ref, blocks, tiles):
        self.list_ref, self.blocks, self.tiles = list_ref, blocks, tiles
        self.room = (list_ref.shape[0] - 1) // 2

    def each(self, step, unroll=1, tail=1):
        def one(pair):
            b = self.list_ref[pair]
            k = self.list_ref[self.room + pair]
            step(jnp.minimum(b, self.blocks - 1), jnp.minimum(k, self.tiles - 1), b, k)

        def groups(first, last, size, start):
            def group(index, carry):
                for u in range(size):
                    one(start + index * size + u)
                return carry

            lax.fori_loop(first, last, group, 0)

        count = self.list_ref[2 * self.room]
        whole = lax.div(count, unroll)
        groups(0, whole, unroll, 0)
        if unroll > tail:
            start = whole * unroll
            groups(0, lax.div(count - start + tail - 1, tail), tail, start)


def at(index, size):
    if isinstance(index, int):
        return pl.ds(index * size, size)
    return pl.ds(pl.multiple_of(index * size, size), size)


def inner_of(right_ref, left_ref, b, k):
    dim = left_ref.shape[0]
    return jnp.dot(
        right_ref[at(k, TILE), :][:, :dim], left_ref[:, at(b, TILE)], preferred_element_type=f32
    )


def half(x, h):
    return x[:, h * LANES : (h + 1) * LANES]


def by_eights(x, op):
    return op(x.reshape(x.shape[0] // 8, 8, x.shape[1]), axis=0)


def row_of(ref, b, h):
    return ref[pl.ds(b * HALVES + h, 1), :]


def gather_columns(acc_ref, tiles, out_ref, op):
    for k in range(tiles):
        for h in range(HALVES):
            part = acc_ref[k, h * LANES : (h + 1) * LANES, :].T
            row = k * HALVES + h
            out_ref[row : row + 1, :] = op(part, axis=0, keepdims=True)


def gather_rows(acc_ref, blocks, out_ref, op):
    for b in range(blocks):
        part = op(acc_ref[b], axis=0, keepdims=True)
        for h in range(HALVES):
            row = b * HALVES + h
            out_ref[row : row + 1, :] = half(part, h)


def col_scores(
    weight, pot, left_norm, right_norm, right_ref, left_ref, pairs, scr, out_ref
):
    dim = left_ref.shape[0]
    scale = 1.0 / (dim * eps)
    vec_ref, vec2_ref, _, _, acc_ref, col_ref, col2_ref = scr
    terms = weight + pot * (1.0 / eps)
    alpha = (terms - left_norm * (0.5 * scale)) * log2e
    top = jnp.max(alpha, keepdims=True)
    alpha = alpha - top
    rows = alpha.shape[0]
    acc_ref[...] = jnp.zeros(acc_ref.shape, f32)

    def add(b, k, to_b, to_k):
        z = inner_of(right_ref, left_ref, b, k) * (scale * log2e)
        parts = [jnp.exp2(half(z, h) + row_of(vec_ref, b, h)) for h in range(HALVES)]
        acc_ref[to_k] += functools.reduce(jnp.add, parts)

    vec_ref[0:rows, :] = alpha
    pairs.each(add, UNROLL, TAIL)
    gather_columns(acc_ref, pairs.tiles, out_ref, jnp.sum)
    total = out_ref[...]
    out_ref[...] = jnp.log(total) + top * ln2 - right_norm * (0.5 * scale)

    @pl.when(jnp.logical_not(in_range(total)))
    def _():
        vec_ref[0:rows, :] = terms
        vec2_ref[0:rows, :] = left_norm
        to_columns(right_norm, col_ref)
        acc_ref[...] = jnp.full(acc_ref.shape, very_low, f32)

        def scores(b, k):
            z = inner_of(right_ref, left_ref, b, k)
            tgt = col_ref[at(k, TILE), :]
            for h in range(HALVES):
                cost = (row_of(vec2_ref, b, h) + tgt - 2.0 * half(z, h)) * (1.0 / (2.0 * dim))
                yield row_of(vec_ref, b, h) - cost * (1.0 / eps)

        def highest(b, k, to_b, to_k):
            acc_ref[to_k] = functools.reduce(jnp.maximum, scores(b, k), acc_ref[to_k])

        pairs.each(highest)
        gather_columns(acc_ref, pairs.tiles, out_ref, jnp.max)
        peak = out_ref[...]
        to_columns(peak, col2_ref)
        acc_ref[...] = jnp.zeros(acc_ref.shape, f32)

        def add_exact(b, k, to_b, to_k):
            peaks = col2_ref[at(k, TILE), :]
            parts = [jnp.exp(s - peaks) for s in scores(b, k)]
            acc_ref[to_k] += functools.reduce(jnp.add, parts)

        pairs.each(add_exact)
        gather_columns(acc_ref, pairs.tiles, out_ref, jnp.sum)
        out_ref[...] = peak + jnp.log(out_ref[...])


def row_scores(
    weight, pot, right_norm, left_norm, right_ref, left_ref, pairs, scr, out_ref
):
    dim = left_ref.shape[0]
    scale = 1.0 / (dim * eps)
    vec_ref, vec2_ref, acc_ref, _, _, col_ref, col2_ref = scr
    terms = weight + pot * (1.0 / eps)
    beta = (terms - right_norm * (0.5 * scale)) * log2e
    top = jnp.max(beta, keepdims=True)
    beta = beta - top
    acc_ref[...] = jnp.zeros(acc_ref.shape, f32)

    def add(b, k, to_b, to_k):
        z = inner_of(right_ref, left_ref, b, k) * (scale * log2e)
        tgt = col_ref[at(k, TILE), :]
        for h in range(HALVES):
            part = by_eights(jnp.exp2(half(z, h) + tgt), jnp.sum)
            acc_ref[to_b, :, h * LANES : (h + 1) * LANES] += part

    to_columns(beta, col_ref)
    pairs.each(add, UNROLL, TAIL)
    gather_rows(acc_ref, pairs.blocks, out_ref, jnp.sum)
    total = out_ref[...]
    out_ref[...] = jnp.log(total) + top * ln2 - left_norm * (0.5 * scale)

    @pl.when(jnp.logical_not(in_range(total)))
    def _():
        rows = left_norm.shape[0]
        to_columns(terms, col_ref)
        to_columns(right_norm, col2_ref)
        vec_ref[0:rows, :] = left_norm
        acc_ref[...] = jnp.full(acc_ref.shape, very_low, f32)

        def scores(b, k):
            z = inner_of(right_ref, left_ref, b, k)
            for h in range(HALVES):
                cost = (row_of(vec_ref, b, h) + col2_ref[at(k, TILE), :] - 2.0 * half(z, h)) * (
                    1.0 / (2.0 * dim)
                )
                yield col_ref[at(k, TILE), :] - cost * (1.0 / eps)

        def highest(b, k, to_b, to_k):
            for h, s in enumerate(scores(b, k)):
                where = slice(h * LANES, (h + 1) * LANES)
                acc_ref[to_b, :, where] = jnp.maximum(
                    acc_ref[to_b, :, where], by_eights(s, jnp.max)
                )

        pairs.each(highest)
        gather_rows(acc_ref, pairs.blocks, out_ref, jnp.max)
        peak = out_ref[...]
        vec2_ref[0:rows, :] = peak
        acc_ref[...] = jnp.zeros(acc_ref.shape, f32)

        def add_exact(b, k, to_b, to_k):
            for h, s in enumerate(scores(b, k)):
                where = slice(h * LANES, (h + 1) * LANES)
                acc_ref[to_b, :, where] += by_eights(
                    jnp.exp(s - row_of(vec2_ref, b, h)), jnp.sum
                )

        pairs.each(add_exact)
        gather_rows(acc_ref, pairs.blocks, out_ref, jnp.sum)
        out_ref[...] = peak + jnp.log(out_ref[...])


def look_up(table, which, out_ref):
    table = table.T
    high = table.astype(bf16)
    rest = table - high.astype(f32)
    middle = rest.astype(bf16)
    low = (rest - middle.astype(f32)).astype(bf16)
    upper = jnp.concatenate([high, middle], axis=1)
    place = lax.broadcasted_iota(jnp.int32, (LANES, TILE), 0)
    for row in range(0, which.shape[0], HALVES):
        index = jnp.concatenate([which[row + h : row + h + 1, :] for h in range(HALVES)], axis=1)
        hot = jnp.where(place == lax.shift_right_logical(index, 7), 1.0, 0.0).astype(bf16)
        value = jnp.dot(upper, jnp.concatenate([hot, hot], axis=0), preferred_element_type=f32)
        value = value + jnp.dot(low, hot, preferred_element_type=f32)
        value = jnp.where(place == jnp.bitwise_and(index, LANES - 1), value, 0.0)
        value = jnp.sum(value, axis=0, keepdims=True)
        for h in range(HALVES):
            out_ref[row + h : row + h + 1, :] = half(value, h)


def to_all(out_ref, value, start=0):
    out_ref[:, start : start + value.shape[0], :] = jnp.broadcast_to(
        value[None], (out_ref.shape[0],) + value.shape
    )


def coarse_start(src_ref, tgt_ref, from_ref, send_ref, *scr):
    *scr, out_ref, left_ref, points_ref, weight_ref, right_ref, ln_ref, rn_ref, sems = scr
    moves = ((src_ref, left_ref), (tgt_ref, points_ref), (from_ref, weight_ref))
    copies = [pltpu.make_async_copy(a, b, sems.at[i]) for i, (a, b) in enumerate(moves)]
    for copy in copies:
        copy.start()
    for copy in copies:
        copy.wait()
    prepare_points(left_ref, points_ref, right_ref, ln_ref, rn_ref)
    pairs = Static(left_ref.shape[1] // TILE, points_ref.shape[1] // TILE)
    weight = weight_ref[...]
    pot = jnp.zeros(weight.shape, f32)
    col_scores(weight, pot, ln_ref[...], rn_ref[...], right_ref, left_ref, pairs, scr, out_ref)
    to_all(send_ref, out_ref[...])


def coarse_rows_first(
    left_ref, points_ref, from_ref, right_ref, ln_ref, rn_ref, weight_ref, out_ref, *scr
):
    prepare_points(left_ref, points_ref, right_ref, ln_ref, rn_ref)
    weight = from_ref[...]
    weight_ref[...] = weight
    pairs = Static(left_ref.shape[1] // TILE, right_ref.shape[0] // TILE)
    pot = jnp.zeros(weight.shape, f32)
    row_scores(weight, pot, rn_ref[...], ln_ref[...], right_ref, left_ref, pairs, scr, out_ref)


def coarse_rows_second(
    recv_ref, first_ref, left_ref, right_ref, ln_ref, rn_ref, weight_ref, send_ref, tgt_ref, *scr
):
    *scr, out_ref = scr
    tgt = (-0.5 * eps) * combine(recv_ref[...])
    tgt_ref[...] = tgt
    pairs = Static(left_ref.shape[1] // TILE, right_ref.shape[0] // TILE)
    row_scores(
        weight_ref[...], tgt, rn_ref[...], ln_ref[...], right_ref, left_ref, pairs, scr, out_ref
    )
    first = first_ref[...]
    to_all(send_ref, first)
    to_all(send_ref, out_ref[...], first.shape[0])


def coarse_cols(
    recv_ref, left_ref, right_ref, ln_ref, rn_ref, weight_ref, after_ref, send_ref, *scr
):
    *scr, out_ref = scr
    lse = combine(recv_ref[...])
    rows = lse.shape[0] // 2
    first = (-0.5 * eps) * lse[:rows]
    second = 0.5 * (first - eps * lse[rows:])
    to_all(send_ref, second)
    pairs = Static(left_ref.shape[1] // TILE, right_ref.shape[0] // TILE)
    col_scores(
        weight_ref[...], first, ln_ref[...], rn_ref[...], right_ref, left_ref, pairs, scr, out_ref
    )
    to_all(send_ref, out_ref[...], rows)


def coarse_end(recv_ref, tgt_ref, send_ref):
    count = tgt_ref.shape[0]
    rows = recv_ref.shape[1] - count
    lse = combine(recv_ref[:, rows:, :])
    to_all(send_ref, 0.5 * (tgt_ref[...] - eps * lse))


def prepare(
    left_ref, points_ref, support_ref, counts_ref, after_ref, right_ref, ln_ref, rn_ref, list_ref
):
    blocks = left_ref.shape[1] // TILE
    tiles = points_ref.shape[1] // TILE
    most = support_ref.shape[2]
    room = (list_ref.shape[0] - 1) // 2

    def one_block(b, found):
        count = counts_ref[b, 0]
        for m in range(most):
            list_ref[found] = b
            list_ref[room + found] = support_ref[b, 0, m]
            found = found + jnp.where(m < count, 1, 0)
        return found

    found = lax.fori_loop(0, blocks, one_block, 0)
    for u in range(TAIL):
        list_ref[found + u] = blocks
        list_ref[room + found + u] = tiles
    list_ref[2 * room] = found
    prepare_points(left_ref, points_ref, right_ref, ln_ref, rn_ref)


def fine_cols_first(
    list_ref, recv_ref, which_ref, left_ref, right_ref, ln_ref, rn_ref, weight_ref, send_ref, src_ref, *scr
):
    *scr, table_ref, out_ref = scr
    shards = recv_ref.shape[0]
    rows = table_ref.shape[0] // shards
    for shard in range(shards):
        table_ref[shard * rows : (shard + 1) * rows, :] = recv_ref[shard, 0:rows, :]
    look_up(table_ref[...], which_ref[...], src_ref)
    pairs = Listed(list_ref, left_ref.shape[1] // TILE, right_ref.shape[0] // TILE)
    col_scores(
        weight_ref[...], src_ref[...], ln_ref[...], rn_ref[...], right_ref, left_ref, pairs, scr, out_ref
    )
    to_all(send_ref, out_ref[...])


def fine_rows_first(
    list_ref, recv_ref, which_ref, left_ref, right_ref, ln_ref, rn_ref, weight_ref, out_ref, tgt_ref, *scr
):
    *scr, table_ref = scr
    shards = recv_ref.shape[0]
    rows = table_ref.shape[0] // shards
    for shard in range(shards):
        table_ref[shard * rows : (shard + 1) * rows, :] = recv_ref[shard]
    look_up(table_ref[...], which_ref[...], tgt_ref)
    pairs = Listed(list_ref, left_ref.shape[1] // TILE, right_ref.shape[0] // TILE)
    row_scores(
        weight_ref[...], tgt_ref[...], rn_ref[...], ln_ref[...], right_ref, left_ref, pairs, scr, out_ref
    )


def fine_rows_second(
    list_ref, recv_ref, tgt_ref, first_ref, left_ref, right_ref, ln_ref, rn_ref, weight_ref, send_ref, new_ref, *scr
):
    *scr, out_ref = scr
    new_ref[...] = 0.5 * (tgt_ref[...] - eps * combine(recv_ref[...]))
    pairs = Listed(list_ref, left_ref.shape[1] // TILE, right_ref.shape[0] // TILE)
    row_scores(
        weight_ref[...], new_ref[...], rn_ref[...], ln_ref[...], right_ref, left_ref, pairs, scr, out_ref
    )
    shards, rows, _ = send_ref.shape
    rows = rows // 2
    for shard in range(shards):
        where = slice(shard * rows, (shard + 1) * rows)
        send_ref[shard, 0:rows, :] = first_ref[where, :]
        send_ref[shard, rows : 2 * rows, :] = out_ref[where, :]


def combine_rows(recv_ref, send_ref):
    to_all(send_ref, combine(recv_ref[...]))


def fine_cols_second(
    list_ref, recv_ref, src_ref, left_ref, right_ref, ln_ref, rn_ref, weight_ref, send_ref, *scr
):
    *scr, first_ref, out_ref = scr
    shards, rows, _ = recv_ref.shape
    rows = rows // 2
    for shard in range(shards):
        where = slice(shard * rows, (shard + 1) * rows)
        first_ref[where, :] = 0.5 * (src_ref[where, :] - eps * recv_ref[shard, 0:rows, :])
    pairs = Listed(list_ref, left_ref.shape[1] // TILE, right_ref.shape[0] // TILE)
    col_scores(
        weight_ref[...], first_ref[...], ln_ref[...], rn_ref[...], right_ref, left_ref, pairs, scr, out_ref
    )
    to_all(send_ref, out_ref[...])


def fine_end(rows_ref, src_ref, recv_ref, tgt_ref, src_out_ref, tgt_out_ref):
    shards, rows, _ = rows_ref.shape
    rows = rows // 2
    for shard in range(shards):
        where = slice(shard * rows, (shard + 1) * rows)
        first = 0.5 * (src_ref[where, :] - eps * rows_ref[shard, 0:rows, :])
        src_out_ref[where, :] = 0.5 * (first - eps * rows_ref[shard, rows : 2 * rows, :])
    tgt_out_ref[...] = 0.5 * (tgt_ref[...] - eps * combine(recv_ref[...]))


def scratch_for(left, right, spare):
    rows = left // LANES
    return [
        pltpu.VMEM((rows, LANES), f32),
        pltpu.VMEM((rows, LANES), f32),
        pltpu.VMEM((left // TILE + spare, 8, TILE), f32),
        pltpu.VMEM((8, LANES), f32),
        pltpu.VMEM((right // TILE + spare, TILE, LANES), f32),
        pltpu.VMEM((right, LANES), f32),
        pltpu.VMEM((right, LANES), f32),
    ]


def call(body, outs, operands, scratch=(), smem=(), smem_out=(), hbm=(), work=0, limit=24):
    spaces = [
        pltpu.SMEM if i in smem else pltpu.HBM if i in hbm else pltpu.VMEM for i in range(len(operands))
    ]
    out_spaces = [pltpu.SMEM if i in smem_out else pltpu.VMEM for i in range(len(outs))]
    return pl.pallas_call(
        body,
        out_shape=[jax.ShapeDtypeStruct(shape, dtype) for shape, dtype in outs],
        in_specs=[pl.BlockSpec(memory_space=s) for s in spaces],
        out_specs=[pl.BlockSpec(memory_space=s) for s in out_spaces],
        scratch_shapes=list(scratch),
        compiler_params=pltpu.CompilerParams(vmem_limit_bytes=limit * 1024 * 1024),
        cost_estimate=pl.CostEstimate(
            flops=128 * work + 1000, bytes_accessed=1 << 20, transcendentals=work
        ),
    )(*operands)


def exchange(x, axis):
    return lax.all_to_all(x, axis, 0, 0, tiled=True)


def per_device(
    n_src,
    n_tgt,
    src_centroids,
    tgt_centroids,
    src_weights,
    tgt_weights,
    src_cells,
    tgt_cells,
    src_mass,
    tgt_mass,
    src_cluster,
    tgt_cluster,
    support,
    counts,
):
    cs, ct = src_centroids.shape[1], tgt_centroids.shape[1]
    fs, ft = src_cells.shape[1], tgt_cells.shape[1]
    csr, ctr, fsr, ftr = (n // LANES for n in (cs, ct, fs, ft))
    vec = lambda x: x.reshape(-1, LANES)
    src_weights, tgt_weights, src_mass, tgt_mass, src_cluster, tgt_cluster = map(
        vec, (src_weights, tgt_weights, src_mass, tgt_mass, src_cluster, tgt_cluster)
    )
    coarse_scratch = scratch_for(cs, ct, 0)
    fine_scratch = scratch_for(fs, ft, 1)
    one = lambda rows: pltpu.VMEM((rows, LANES), f32)
    coarse_work = cs * ct
    fine_work = fs * ft // 4

    (send,) = call(
        coarse_start,
        [((n_src, ctr, LANES), f32)],
        [src_centroids, tgt_centroids, src_weights],
        coarse_scratch
        + [
            one(ctr),
            pltpu.VMEM(src_centroids.shape, bf16),
            pltpu.VMEM(tgt_centroids.shape, bf16),
            one(csr),
            pltpu.VMEM((ct, LANES), bf16),
            one(csr),
            one(ctr),
            pltpu.SemaphoreType.DMA((3,)),
        ],
        hbm=(0, 1, 2),
        limit=64,
        work=coarse_work,
    )
    recv = exchange(send, "src")
    right, ln, rn, tgt_weights, first_rows = call(
        coarse_rows_first,
        [
            ((ct, LANES), bf16),
            ((csr, LANES), f32),
            ((ctr, LANES), f32),
            ((ctr, LANES), f32),
            ((csr, LANES), f32),
        ],
        [src_centroids, tgt_centroids, tgt_weights],
        coarse_scratch,
        work=coarse_work,
    )
    send, coarse_tgt = call(
        coarse_rows_second,
        [((n_tgt, 2 * csr, LANES), f32), ((ctr, LANES), f32)],
        [recv, first_rows, src_centroids, right, ln, rn, tgt_weights],
        coarse_scratch + [one(csr)],
        work=coarse_work,
    )
    room = support.shape[0] * support.shape[2] + TAIL
    fine_right, fine_ln, fine_rn, listed = call(
        prepare,
        [
            ((ft, LANES), bf16),
            ((fsr, LANES), f32),
            ((ftr, LANES), f32),
            ((2 * room + 1,), jnp.int32),
        ],
        [src_cells, tgt_cells, support, counts, coarse_tgt],
        smem=(2, 3),
        smem_out=(3,),
        work=2 * coarse_work,
    )
    recv = exchange(send, "tgt")
    (send,) = call(
        coarse_cols,
        [((n_src, csr + ctr, LANES), f32)],
        [recv, src_centroids, right, ln, rn, src_weights, fine_rn],
        coarse_scratch + [one(ctr)],
        work=coarse_work,
    )
    every_src = exchange(send, "src")
    (send,) = call(coarse_end, [((n_tgt, ctr, LANES), f32)], [every_src, coarse_tgt])
    every_tgt = exchange(send, "tgt")

    fine_static = [src_cells, fine_right, fine_ln, fine_rn]
    send, fine_src = call(
        fine_cols_first,
        [((n_src, ftr, LANES), f32), ((fsr, LANES), f32)],
        [listed, every_src, src_cluster, *fine_static, src_mass],
        fine_scratch + [one(n_src * csr), one(ftr)],
        smem=(0,),
        work=fine_work,
    )
    recv = exchange(send, "src")
    first_rows, fine_tgt = call(
        fine_rows_first,
        [((fsr, LANES), f32), ((ftr, LANES), f32)],
        [listed, every_tgt, tgt_cluster, *fine_static, tgt_mass],
        fine_scratch + [one(n_tgt * ctr)],
        smem=(0,),
        work=fine_work,
    )
    send, fine_tgt = call(
        fine_rows_second,
        [((n_tgt, 2 * fsr // n_tgt, LANES), f32), ((ftr, LANES), f32)],
        [listed, recv, fine_tgt, first_rows, *fine_static, tgt_mass],
        fine_scratch + [one(fsr)],
        smem=(0,),
        work=fine_work,
    )
    recv = exchange(send, "tgt")
    (send,) = call(combine_rows, [(recv.shape, f32)], [recv])
    rows = exchange(send, "tgt")
    (send,) = call(
        fine_cols_second,
        [((n_src, ftr, LANES), f32)],
        [listed, rows, fine_src, *fine_static, src_mass],
        fine_scratch + [one(fsr), one(ftr)],
        smem=(0,),
        work=fine_work,
    )
    recv = exchange(send, "src")
    fine_src, fine_tgt = call(
        fine_end,
        [((fsr, LANES), f32), ((ftr, LANES), f32)],
        [rows, fine_src, recv, fine_tgt],
    )
    return (fine_src.reshape(fs), fine_tgt.reshape(ft))


def solution(mesh):
    in_specs = (
        P(None, "src"),
        P(None, "tgt"),
        P("src"),
        P("tgt"),
        P(None, "src"),
        P(None, "tgt"),
        P("src"),
        P("tgt"),
        P("src"),
        P("tgt"),
        P("src", "tgt", None),
        P("src", "tgt"),
    )
    out_specs = (P("src"), P("tgt"))
    body = functools.partial(per_device, mesh.shape["src"], mesh.shape["tgt"])
    return jax.shard_map(body, mesh=mesh, in_specs=in_specs, out_specs=out_specs, check_vma=False)
```

```python
import functools
import math
import jax
import jax.numpy as jnp
from jax import lax
from jax.experimental import pallas as pl
from jax.experimental.pallas import tpu as pltpu
from jax.sharding import PartitionSpec as P

TILE = 256
LANES = 128
HALVES = TILE // LANES
UNROLL = 32
TAIL = 16
CHUNK = 8
CHUNKS = 5
PAIRS_A_CHUNK = 20

eps = 0.0625
log2e = math.log2(math.e)
ln2 = math.log(2.0)
smallest = 1e-25
largest = 1e37
farthest = -120.0
very_low = -3e38

f32 = jnp.float32
bf16 = jnp.bfloat16


def norms_of(points_ref, out_ref):
    for row in range(out_ref.shape[0]):
        part = points_ref[:, row * LANES : (row + 1) * LANES].astype(f32)
        out_ref[row : row + 1, :] = jnp.sum(part * part, axis=0, keepdims=True)


def transpose_points(points_ref, out_ref):
    dim, count = points_ref.shape
    for start in range(0, count, LANES):
        part = points_ref[:, start : start + LANES].astype(f32)
        part = jnp.concatenate([part, jnp.zeros((LANES - dim, LANES), f32)], axis=0)
        out_ref[start : start + LANES, :] = part.T.astype(bf16)


def to_columns(rows, out_ref):
    for row in range(rows.shape[0]):
        spread = jnp.broadcast_to(rows[row : row + 1, :], (LANES, LANES))
        out_ref[row * LANES : (row + 1) * LANES, :] = spread.T


def prepare_points(left_ref, points_ref, right_ref, ln_ref, rn_ref):
    norms_of(left_ref, ln_ref)
    norms_of(points_ref, rn_ref)
    transpose_points(points_ref, right_ref)


def combine(parts):
    peak = jnp.max(parts, axis=0)
    return peak + jnp.log(jnp.sum(jnp.exp(parts - peak[None]), axis=0))


def in_range(total, own):
    total_fits = jnp.logical_and(jnp.min(total) >= smallest, jnp.max(total) <= largest)
    return jnp.logical_and(total_fits, jnp.min(own) >= farthest)


class Static:
    def __init__(self, blocks, tiles):
        self.blocks, self.tiles = blocks, tiles

    def each_fast(self, step, step_held):
        self.each(step)

    def each(self, step):
        for b in range(self.blocks):
            for k in range(self.tiles):
                step(b, k, b, k)


class Listed:
    def __init__(self, list_ref, blocks, tiles, stored_ref=None, held_ref=None, sems=None):
        self.list_ref, self.blocks, self.tiles = list_ref, blocks, tiles
        self.held_ref = held_ref
        self.room = (list_ref.shape[0] - 2) // 2
        self.count = list_ref[2 * self.room]
        self.chunks = list_ref[2 * self.room + 1]
        self.copies = []
        if stored_ref is not None:
            for chunk in range(CHUNKS):
                where = pl.ds(chunk * CHUNK, CHUNK)
                self.copies.append(
                    pltpu.make_async_copy(stored_ref.at[where], held_ref.at[where], sems.at[chunk])
                )
                pl.when(chunk < self.chunks)(self.copies[-1].start)

    def of(self, pair):
        return self.list_ref[pair], self.list_ref[self.room + pair]

    def clip(self, b, k):
        return jnp.minimum(b, self.blocks - 1), jnp.minimum(k, self.tiles - 1)

    def each(self, step, unroll=1, tail=1, first=0):
        def groups(number, size, start):
            def group(index, carry):
                for u in range(size):
                    b, k = self.of(start + index * size + u)
                    step(*self.clip(b, k), b, k)
                return carry

            lax.fori_loop(0, number, group, 0)

        count = self.count - first
        whole = lax.div(count, unroll)
        groups(whole, unroll, first)
        if unroll > tail:
            done = whole * unroll
            groups(lax.div(count - done + tail - 1, tail), tail, first + done)

    def each_fast(self, step, step_held):
        if not self.copies:
            return self.each(step, UNROLL, TAIL)
        self.each(step, UNROLL, TAIL, self.chunks * CHUNK)
        for chunk, copy in enumerate(self.copies):

            @pl.when(chunk < self.chunks)
            def _():
                copy.wait()
                for pair in range(chunk * CHUNK, (chunk + 1) * CHUNK):
                    step_held(self.held_ref.at[pair], *self.of(pair))


def at(index, size):
    if isinstance(index, int):
        return pl.ds(index * size, size)
    return pl.ds(pl.multiple_of(index * size, size), size)


def inner_of(right_ref, left_ref, b, k):
    dim = left_ref.shape[0]
    return jnp.dot(
        right_ref[at(k, TILE), :][:, :dim], left_ref[:, at(b, TILE)], preferred_element_type=f32
    )


def half(x, h):
    return x[:, h * LANES : (h + 1) * LANES]


def by_eights(x, op):
    return op(x.reshape(x.shape[0] // 8, 8, x.shape[1]), axis=0)


def row_of(ref, b, h):
    return ref[pl.ds(b * HALVES + h, 1), :]


def gather_columns(acc_ref, tiles, out_ref, op):
    for k in range(tiles):
        for h in range(HALVES):
            part = acc_ref[k, h * LANES : (h + 1) * LANES, :].T
            row = k * HALVES + h
            out_ref[row : row + 1, :] = op(part, axis=0, keepdims=True)


def gather_rows(acc_ref, blocks, out_ref, op):
    for b in range(blocks):
        part = op(acc_ref[b], axis=0, keepdims=True)
        for h in range(HALVES):
            row = b * HALVES + h
            out_ref[row : row + 1, :] = half(part, h)


def col_scores(
    weight, pot, left_norm, right_norm, right_ref, left_ref, pairs, scr, out_ref
):
    dim = left_ref.shape[0]
    scale = 1.0 / (dim * eps)
    vec_ref, vec2_ref, _, _, acc_ref, col_ref, col2_ref = scr
    terms = weight + pot * (1.0 / eps)
    alpha = (terms - left_norm * (0.5 * scale)) * log2e
    top = jnp.max(alpha, keepdims=True)
    alpha = alpha - top
    rows = alpha.shape[0]
    acc_ref[...] = jnp.zeros(acc_ref.shape, f32)

    def add(b, k, to_b, to_k):
        z = inner_of(right_ref, left_ref, b, k) * (scale * log2e)
        parts = [jnp.exp2(half(z, h) + row_of(vec_ref, b, h)) for h in range(HALVES)]
        acc_ref[to_k] += functools.reduce(jnp.add, parts)

    vec_ref[0:rows, :] = alpha
    vec2_ref[0:rows, :] = jnp.exp2(alpha)

    def add_held(e_ref, b, k):
        parts = [
            e_ref[:, h * LANES : (h + 1) * LANES] * row_of(vec2_ref, b, h) for h in range(HALVES)
        ]
        acc_ref[k] += functools.reduce(jnp.add, parts)

    pairs.each_fast(add, add_held)
    gather_columns(acc_ref, pairs.tiles, out_ref, jnp.sum)
    total = out_ref[...]
    out_ref[...] = jnp.log(total) + top * ln2 - right_norm * (0.5 * scale)

    @pl.when(jnp.logical_not(in_range(total, alpha)))
    def _():
        vec_ref[0:rows, :] = terms
        vec2_ref[0:rows, :] = left_norm
        to_columns(right_norm, col_ref)
        acc_ref[...] = jnp.full(acc_ref.shape, very_low, f32)

        def scores(b, k):
            z = inner_of(right_ref, left_ref, b, k)
            tgt = col_ref[at(k, TILE), :]
            for h in range(HALVES):
                cost = (row_of(vec2_ref, b, h) + tgt - 2.0 * half(z, h)) * (1.0 / (2.0 * dim))
                yield row_of(vec_ref, b, h) - cost * (1.0 / eps)

        def highest(b, k, to_b, to_k):
            acc_ref[to_k] = functools.reduce(jnp.maximum, scores(b, k), acc_ref[to_k])

        pairs.each(highest)
        gather_columns(acc_ref, pairs.tiles, out_ref, jnp.max)
        peak = out_ref[...]
        to_columns(peak, col2_ref)
        acc_ref[...] = jnp.zeros(acc_ref.shape, f32)

        def add_exact(b, k, to_b, to_k):
            peaks = col2_ref[at(k, TILE), :]
            parts = [jnp.exp(s - peaks) for s in scores(b, k)]
            acc_ref[to_k] += functools.reduce(jnp.add, parts)

        pairs.each(add_exact)
        gather_columns(acc_ref, pairs.tiles, out_ref, jnp.sum)
        out_ref[...] = peak + jnp.log(out_ref[...])


def row_scores(
    weight, pot, right_norm, left_norm, right_ref, left_ref, pairs, scr, out_ref
):
    dim = left_ref.shape[0]
    scale = 1.0 / (dim * eps)
    vec_ref, vec2_ref, acc_ref, _, _, col_ref, col2_ref = scr
    terms = weight + pot * (1.0 / eps)
    beta = (terms - right_norm * (0.5 * scale)) * log2e
    top = jnp.max(beta, keepdims=True)
    beta = beta - top
    acc_ref[...] = jnp.zeros(acc_ref.shape, f32)

    def add(b, k, to_b, to_k):
        z = inner_of(right_ref, left_ref, b, k) * (scale * log2e)
        tgt = col_ref[at(k, TILE), :]
        for h in range(HALVES):
            part = by_eights(jnp.exp2(half(z, h) + tgt), jnp.sum)
            acc_ref[to_b, :, h * LANES : (h + 1) * LANES] += part

    to_columns(beta, col_ref)
    col2_ref[...] = jnp.exp2(col_ref[...])
    def add_held(e_ref, b, k):
        tgt = col2_ref[at(k, TILE), :]
        for h in range(HALVES):
            where = slice(h * LANES, (h + 1) * LANES)
            acc_ref[b, :, where] += by_eights(e_ref[:, where] * tgt, jnp.sum)

    pairs.each_fast(add, add_held)
    gather_rows(acc_ref, pairs.blocks, out_ref, jnp.sum)
    total = out_ref[...]
    out_ref[...] = jnp.log(total) + top * ln2 - left_norm * (0.5 * scale)

    @pl.when(jnp.logical_not(in_range(total, beta)))
    def _():
        rows = left_norm.shape[0]
        to_columns(terms, col_ref)
        to_columns(right_norm, col2_ref)
        vec_ref[0:rows, :] = left_norm
        acc_ref[...] = jnp.full(acc_ref.shape, very_low, f32)

        def scores(b, k):
            z = inner_of(right_ref, left_ref, b, k)
            for h in range(HALVES):
                cost = (row_of(vec_ref, b, h) + col2_ref[at(k, TILE), :] - 2.0 * half(z, h)) * (
                    1.0 / (2.0 * dim)
                )
                yield col_ref[at(k, TILE), :] - cost * (1.0 / eps)

        def highest(b, k, to_b, to_k):
            for h, s in enumerate(scores(b, k)):
                where = slice(h * LANES, (h + 1) * LANES)
                acc_ref[to_b, :, where] = jnp.maximum(
                    acc_ref[to_b, :, where], by_eights(s, jnp.max)
                )

        pairs.each(highest)
        gather_rows(acc_ref, pairs.blocks, out_ref, jnp.max)
        peak = out_ref[...]
        vec2_ref[0:rows, :] = peak
        acc_ref[...] = jnp.zeros(acc_ref.shape, f32)

        def add_exact(b, k, to_b, to_k):
            for h, s in enumerate(scores(b, k)):
                where = slice(h * LANES, (h + 1) * LANES)
                acc_ref[to_b, :, where] += by_eights(
                    jnp.exp(s - row_of(vec2_ref, b, h)), jnp.sum
                )

        pairs.each(add_exact)
        gather_rows(acc_ref, pairs.blocks, out_ref, jnp.sum)
        out_ref[...] = peak + jnp.log(out_ref[...])


def look_up(table, which, out_ref):
    table = table.T
    high = table.astype(bf16)
    rest = table - high.astype(f32)
    middle = rest.astype(bf16)
    low = (rest - middle.astype(f32)).astype(bf16)
    upper = jnp.concatenate([high, middle], axis=1)
    place = lax.broadcasted_iota(jnp.int32, (LANES, TILE), 0)
    for row in range(0, which.shape[0], HALVES):
        index = jnp.concatenate([which[row + h : row + h + 1, :] for h in range(HALVES)], axis=1)
        hot = jnp.where(place == lax.shift_right_logical(index, 7), 1.0, 0.0).astype(bf16)
        value = jnp.dot(upper, jnp.concatenate([hot, hot], axis=0), preferred_element_type=f32)
        value = value + jnp.dot(low, hot, preferred_element_type=f32)
        value = jnp.where(place == jnp.bitwise_and(index, LANES - 1), value, 0.0)
        value = jnp.sum(value, axis=0, keepdims=True)
        for h in range(HALVES):
            out_ref[row + h : row + h + 1, :] = half(value, h)


def to_all(out_ref, value, start=0):
    out_ref[:, start : start + value.shape[0], :] = jnp.broadcast_to(
        value[None], (out_ref.shape[0],) + value.shape
    )


def coarse_start(src_ref, tgt_ref, from_ref, send_ref, *scr):
    *scr, out_ref, left_ref, points_ref, weight_ref, right_ref, ln_ref, rn_ref, sems = scr
    moves = ((src_ref, left_ref), (tgt_ref, points_ref), (from_ref, weight_ref))
    copies = [pltpu.make_async_copy(a, b, sems.at[i]) for i, (a, b) in enumerate(moves)]
    for copy in copies:
        copy.start()
    for copy in copies:
        copy.wait()
    prepare_points(left_ref, points_ref, right_ref, ln_ref, rn_ref)
    pairs = Static(left_ref.shape[1] // TILE, points_ref.shape[1] // TILE)
    weight = weight_ref[...]
    pot = jnp.zeros(weight.shape, f32)
    col_scores(weight, pot, ln_ref[...], rn_ref[...], right_ref, left_ref, pairs, scr, out_ref)
    to_all(send_ref, out_ref[...])


def coarse_rows_first(
    src_ref, points_ref, from_ref, left_ref, right_ref, ln_ref, rn_ref, weight_ref, out_ref, *scr
):
    left_ref[...] = src_ref[...]
    prepare_points(left_ref, points_ref, right_ref, ln_ref, rn_ref)
    weight = from_ref[...]
    weight_ref[...] = weight
    pairs = Static(left_ref.shape[1] // TILE, right_ref.shape[0] // TILE)
    pot = jnp.zeros(weight.shape, f32)
    row_scores(weight, pot, rn_ref[...], ln_ref[...], right_ref, left_ref, pairs, scr, out_ref)


def coarse_rows_second(
    recv_ref, first_ref, left_ref, right_ref, ln_ref, rn_ref, weight_ref, send_ref, tgt_ref, *scr
):
    *scr, out_ref = scr
    tgt = (-0.5 * eps) * combine(recv_ref[...])
    tgt_ref[...] = tgt
    pairs = Static(left_ref.shape[1] // TILE, right_ref.shape[0] // TILE)
    row_scores(
        weight_ref[...], tgt, rn_ref[...], ln_ref[...], right_ref, left_ref, pairs, scr, out_ref
    )
    first = first_ref[...]
    to_all(send_ref, first)
    to_all(send_ref, out_ref[...], first.shape[0])


def coarse_cols(
    recv_ref, left_ref, right_ref, ln_ref, rn_ref, weight_ref, after_ref, send_ref, done_ref, *scr
):
    *scr, out_ref = scr
    done_ref[...] = jnp.zeros(done_ref.shape, f32)
    lse = combine(recv_ref[...])
    rows = lse.shape[0] // 2
    first = (-0.5 * eps) * lse[:rows]
    second = 0.5 * (first - eps * lse[rows:])
    to_all(send_ref, second)
    pairs = Static(left_ref.shape[1] // TILE, right_ref.shape[0] // TILE)
    col_scores(
        weight_ref[...], first, ln_ref[...], rn_ref[...], right_ref, left_ref, pairs, scr, out_ref
    )
    to_all(send_ref, out_ref[...], rows)


def store_some(list_ref, left_ref, right_ref, after_ref, stored_ref, done_ref, held_ref, sems):
    done_ref[...] = after_ref[...]
    dim = left_ref.shape[0]
    pairs = Listed(list_ref, left_ref.shape[1] // TILE, right_ref.shape[0] // TILE)
    for wait in (False, True):
        for chunk in range(CHUNKS):
            where = pl.ds(chunk * CHUNK, CHUNK)
            copy = pltpu.make_async_copy(held_ref.at[where], stored_ref.at[where], sems.at[chunk])

            @pl.when(chunk < pairs.chunks)
            def _():
                if wait:
                    copy.wait()
                    return
                for pair in range(chunk * CHUNK, (chunk + 1) * CHUNK):
                    z = inner_of(right_ref, left_ref, *pairs.of(pair))
                    held_ref[pair] = jnp.exp2(z * (log2e / (dim * eps)))
                copy.start()


def coarse_end(recv_ref, tgt_ref, after_ref, send_ref):
    count = tgt_ref.shape[0]
    rows = recv_ref.shape[1] - count
    lse = combine(recv_ref[:, rows:, :])
    to_all(send_ref, 0.5 * (tgt_ref[...] - eps * lse))


def prepare(
    left_ref, points_ref, support_ref, counts_ref, after_ref, right_ref, ln_ref, rn_ref, list_ref
):
    blocks = left_ref.shape[1] // TILE
    tiles = points_ref.shape[1] // TILE
    most = support_ref.shape[2]
    room = (list_ref.shape[0] - 2) // 2

    def one_block(b, found):
        count = counts_ref[b, 0]
        for m in range(most):
            list_ref[found] = b
            list_ref[room + found] = support_ref[b, 0, m]
            found = found + jnp.where(m < count, 1, 0)
        return found

    found = lax.fori_loop(0, blocks, one_block, 0)
    for u in range(TAIL):
        list_ref[found + u] = blocks
        list_ref[room + found + u] = tiles
    list_ref[2 * room] = found
    list_ref[2 * room + 1] = jnp.minimum(lax.div(found, PAIRS_A_CHUNK), CHUNKS)
    prepare_points(left_ref, points_ref, right_ref, ln_ref, rn_ref)


def fine_cols_first(
    list_ref, stored_ref, recv_ref, which_ref, left_ref, right_ref, ln_ref, rn_ref, weight_ref, send_ref, src_ref, *scr
):
    *scr, table_ref, out_ref, held_ref, sems = scr
    pairs = Listed(
        list_ref, left_ref.shape[1] // TILE, right_ref.shape[0] // TILE, stored_ref, held_ref, sems
    )
    shards = recv_ref.shape[0]
    rows = table_ref.shape[0] // shards
    for shard in range(shards):
        table_ref[shard * rows : (shard + 1) * rows, :] = recv_ref[shard, 0:rows, :]
    look_up(table_ref[...], which_ref[...], src_ref)
    col_scores(
        weight_ref[...], src_ref[...], ln_ref[...], rn_ref[...], right_ref, left_ref, pairs, scr, out_ref
    )
    to_all(send_ref, out_ref[...])


def fine_rows_first(
    list_ref, stored_ref, recv_ref, which_ref, left_ref, right_ref, ln_ref, rn_ref, weight_ref, out_ref, tgt_ref, *scr
):
    *scr, table_ref, held_ref, sems = scr
    pairs = Listed(
        list_ref, left_ref.shape[1] // TILE, right_ref.shape[0] // TILE, stored_ref, held_ref, sems
    )
    shards = recv_ref.shape[0]
    rows = table_ref.shape[0] // shards
    for shard in range(shards):
        table_ref[shard * rows : (shard + 1) * rows, :] = recv_ref[shard]
    look_up(table_ref[...], which_ref[...], tgt_ref)
    row_scores(
        weight_ref[...], tgt_ref[...], rn_ref[...], ln_ref[...], right_ref, left_ref, pairs, scr, out_ref
    )


def fine_rows_second(
    list_ref, stored_ref, recv_ref, tgt_ref, first_ref, left_ref, right_ref, ln_ref, rn_ref, weight_ref, send_ref, new_ref, *scr
):
    *scr, out_ref, held_ref, sems = scr
    pairs = Listed(
        list_ref, left_ref.shape[1] // TILE, right_ref.shape[0] // TILE, stored_ref, held_ref, sems
    )
    new_ref[...] = 0.5 * (tgt_ref[...] - eps * combine(recv_ref[...]))
    row_scores(
        weight_ref[...], new_ref[...], rn_ref[...], ln_ref[...], right_ref, left_ref, pairs, scr, out_ref
    )
    shards, rows, _ = send_ref.shape
    rows = rows // 2
    for shard in range(shards):
        where = slice(shard * rows, (shard + 1) * rows)
        send_ref[shard, 0:rows, :] = first_ref[where, :]
        send_ref[shard, rows : 2 * rows, :] = out_ref[where, :]


def combine_rows(recv_ref, send_ref):
    to_all(send_ref, combine(recv_ref[...]))


def fine_cols_second(
    list_ref, stored_ref, recv_ref, src_ref, left_ref, right_ref, ln_ref, rn_ref, weight_ref, send_ref, *scr
):
    *scr, first_ref, out_ref, held_ref, sems = scr
    pairs = Listed(
        list_ref, left_ref.shape[1] // TILE, right_ref.shape[0] // TILE, stored_ref, held_ref, sems
    )
    shards, rows, _ = recv_ref.shape
    rows = rows // 2
    for shard in range(shards):
        where = slice(shard * rows, (shard + 1) * rows)
        first_ref[where, :] = 0.5 * (src_ref[where, :] - eps * recv_ref[shard, 0:rows, :])
    col_scores(
        weight_ref[...], first_ref[...], ln_ref[...], rn_ref[...], right_ref, left_ref, pairs, scr, out_ref
    )
    to_all(send_ref, out_ref[...])


def fine_end(rows_ref, src_ref, recv_ref, tgt_ref, src_out_ref, tgt_out_ref):
    shards, rows, _ = rows_ref.shape
    rows = rows // 2
    for shard in range(shards):
        where = slice(shard * rows, (shard + 1) * rows)
        first = 0.5 * (src_ref[where, :] - eps * rows_ref[shard, 0:rows, :])
        src_out_ref[where, :] = 0.5 * (first - eps * rows_ref[shard, rows : 2 * rows, :])
    tgt_out_ref[...] = 0.5 * (tgt_ref[...] - eps * combine(recv_ref[...]))


def scratch_for(left, right, spare):
    rows = left // LANES
    return [
        pltpu.VMEM((rows, LANES), f32),
        pltpu.VMEM((rows, LANES), f32),
        pltpu.VMEM((left // TILE + spare, 8, TILE), f32),
        pltpu.VMEM((8, LANES), f32),
        pltpu.VMEM((right // TILE + spare, TILE, LANES), f32),
        pltpu.VMEM((right, LANES), f32),
        pltpu.VMEM((right, LANES), f32),
    ]


def call(body, outs, operands, scratch=(), smem=(), smem_out=(), hbm=(), hbm_out=(), work=0, limit=24):
    spaces = [
        pltpu.SMEM if i in smem else pltpu.HBM if i in hbm else pltpu.VMEM for i in range(len(operands))
    ]
    out_spaces = [
        pltpu.SMEM if i in smem_out else pltpu.HBM if i in hbm_out else pltpu.VMEM
        for i in range(len(outs))
    ]
    return pl.pallas_call(
        body,
        out_shape=[jax.ShapeDtypeStruct(shape, dtype) for shape, dtype in outs],
        in_specs=[pl.BlockSpec(memory_space=s) for s in spaces],
        out_specs=[pl.BlockSpec(memory_space=s) for s in out_spaces],
        scratch_shapes=list(scratch),
        compiler_params=pltpu.CompilerParams(vmem_limit_bytes=limit * 1024 * 1024),
        cost_estimate=pl.CostEstimate(
            flops=128 * work + 1000, bytes_accessed=1 << 20, transcendentals=work
        ),
    )(*operands)


def exchange(x, axis):
    return lax.all_to_all(x, axis, 0, 0, tiled=True)


def per_device(
    n_src,
    n_tgt,
    src_centroids,
    tgt_centroids,
    src_weights,
    tgt_weights,
    src_cells,
    tgt_cells,
    src_mass,
    tgt_mass,
    src_cluster,
    tgt_cluster,
    support,
    counts,
):
    cs, ct = src_centroids.shape[1], tgt_centroids.shape[1]
    fs, ft = src_cells.shape[1], tgt_cells.shape[1]
    csr, ctr, fsr, ftr = (n // LANES for n in (cs, ct, fs, ft))
    vec = lambda x: x.reshape(-1, LANES)
    src_weights, tgt_weights, src_mass, tgt_mass, src_cluster, tgt_cluster = map(
        vec, (src_weights, tgt_weights, src_mass, tgt_mass, src_cluster, tgt_cluster)
    )
    coarse_scratch = scratch_for(cs, ct, 0)
    fine_scratch = scratch_for(fs, ft, 1)
    one = lambda rows: pltpu.VMEM((rows, LANES), f32)
    coarse_work = cs * ct
    fine_work = fs * ft // 4

    (send,) = call(
        coarse_start,
        [((n_src, ctr, LANES), f32)],
        [src_centroids, tgt_centroids, src_weights],
        coarse_scratch
        + [
            one(ctr),
            pltpu.VMEM(src_centroids.shape, bf16),
            pltpu.VMEM(tgt_centroids.shape, bf16),
            one(csr),
            pltpu.VMEM((ct, LANES), bf16),
            one(csr),
            one(ctr),
            pltpu.SemaphoreType.DMA((3,)),
        ],
        hbm=(0, 1, 2),
        limit=64,
        work=coarse_work,
    )
    recv = exchange(send, "src")
    left, right, ln, rn, tgt_weights, first_rows = call(
        coarse_rows_first,
        [
            (src_centroids.shape, bf16),
            ((ct, LANES), bf16),
            ((csr, LANES), f32),
            ((ctr, LANES), f32),
            ((ctr, LANES), f32),
            ((csr, LANES), f32),
        ],
        [src_centroids, tgt_centroids, tgt_weights],
        coarse_scratch,
        work=coarse_work,
    )
    send, coarse_tgt = call(
        coarse_rows_second,
        [((n_tgt, 2 * csr, LANES), f32), ((ctr, LANES), f32)],
        [recv, first_rows, left, right, ln, rn, tgt_weights],
        coarse_scratch + [one(csr)],
        work=coarse_work,
    )
    room = support.shape[0] * support.shape[2] + TAIL
    fine_right, fine_ln, fine_rn, listed = call(
        prepare,
        [
            ((ft, LANES), bf16),
            ((fsr, LANES), f32),
            ((ftr, LANES), f32),
            ((2 * room + 2,), jnp.int32),
        ],
        [src_cells, tgt_cells, support, counts, coarse_tgt],
        smem=(2, 3),
        smem_out=(3,),
        work=2 * coarse_work,
    )
    recv = exchange(send, "tgt")
    send, done = call(
        coarse_cols,
        [((n_src, csr + ctr, LANES), f32), ((1, LANES), f32)],
        [recv, left, right, ln, rn, src_weights, fine_rn],
        coarse_scratch + [one(ctr)],
        work=coarse_work,
    )
    every_src = exchange(send, "src")
    held = (CHUNKS * CHUNK, TILE, TILE)
    holding = [pltpu.VMEM(held, f32), pltpu.SemaphoreType.DMA((CHUNKS,))]
    stored, done = call(
        store_some,
        [(held, f32), ((1, LANES), f32)],
        [listed, src_cells, fine_right, done],
        holding,
        smem=(0,),
        hbm_out=(0,),
        limit=48,
        work=fine_work // 2,
    )
    (send,) = call(coarse_end, [((n_tgt, ctr, LANES), f32)], [every_src, coarse_tgt, done])
    every_tgt = exchange(send, "tgt")

    fine_static = [src_cells, fine_right, fine_ln, fine_rn]
    send, fine_src = call(
        fine_cols_first,
        [((n_src, ftr, LANES), f32), ((fsr, LANES), f32)],
        [listed, stored, every_src, src_cluster, *fine_static, src_mass],
        fine_scratch + [one(n_src * csr), one(ftr)] + holding,
        smem=(0,),
        hbm=(1,),
        limit=48,
        work=fine_work,
    )
    recv = exchange(send, "src")
    first_rows, fine_tgt = call(
        fine_rows_first,
        [((fsr, LANES), f32), ((ftr, LANES), f32)],
        [listed, stored, every_tgt, tgt_cluster, *fine_static, tgt_mass],
        fine_scratch + [one(n_tgt * ctr)] + holding,
        smem=(0,),
        hbm=(1,),
        limit=48,
        work=fine_work,
    )
    send, fine_tgt = call(
        fine_rows_second,
        [((n_tgt, 2 * fsr // n_tgt, LANES), f32), ((ftr, LANES), f32)],
        [listed, stored, recv, fine_tgt, first_rows, *fine_static, tgt_mass],
        fine_scratch + [one(fsr)] + holding,
        smem=(0,),
        hbm=(1,),
        limit=48,
        work=fine_work,
    )
    recv = exchange(send, "tgt")
    (send,) = call(combine_rows, [(recv.shape, f32)], [recv])
    rows = exchange(send, "tgt")
    (send,) = call(
        fine_cols_second,
        [((n_src, ftr, LANES), f32)],
        [listed, stored, rows, fine_src, *fine_static, src_mass],
        fine_scratch + [one(fsr), one(ftr)] + holding,
        smem=(0,),
        hbm=(1,),
        limit=48,
        work=fine_work,
    )
    recv = exchange(send, "src")
    fine_src, fine_tgt = call(
        fine_end,
        [((fsr, LANES), f32), ((ftr, LANES), f32)],
        [rows, fine_src, recv, fine_tgt],
    )
    return (fine_src.reshape(fs), fine_tgt.reshape(ft))


def solution(mesh):
    in_specs = (
        P(None, "src"),
        P(None, "tgt"),
        P("src"),
        P("tgt"),
        P(None, "src"),
        P(None, "tgt"),
        P("src"),
        P("tgt"),
        P("src"),
        P("tgt"),
        P("src", "tgt", None),
        P("src", "tgt"),
    )
    out_specs = (P("src"), P("tgt"))
    body = functools.partial(per_device, mesh.shape["src"], mesh.shape["tgt"])
    return jax.shard_map(body, mesh=mesh, in_specs=in_specs, out_specs=out_specs, check_vma=False)
```

```python
import functools
import math
import jax
import jax.numpy as jnp
from jax import lax
from jax.experimental import pallas as pl
from jax.experimental.pallas import tpu as pltpu
from jax.sharding import PartitionSpec as P

TILE = 256
LANES = 128
HALVES = TILE // LANES
UNROLL = 32
TAIL = 16

eps = 0.0625
log2e = math.log2(math.e)
ln2 = math.log(2.0)
smallest = 1e-25
largest = 1e37
very_low = -3e38

f32 = jnp.float32
bf16 = jnp.bfloat16


def norms_of(points_ref, out_ref):
    for row in range(out_ref.shape[0]):
        part = points_ref[:, row * LANES : (row + 1) * LANES].astype(f32)
        out_ref[row : row + 1, :] = jnp.sum(part * part, axis=0, keepdims=True)


def transpose_points(points_ref, out_ref):
    dim, count = points_ref.shape
    for start in range(0, count, LANES):
        part = points_ref[:, start : start + LANES].astype(f32)
        part = jnp.concatenate([part, jnp.zeros((LANES - dim, LANES), f32)], axis=0)
        out_ref[start : start + LANES, :] = part.T.astype(bf16)


def to_columns(rows, out_ref):
    for row in range(rows.shape[0]):
        spread = jnp.broadcast_to(rows[row : row + 1, :], (LANES, LANES))
        out_ref[row * LANES : (row + 1) * LANES, :] = spread.T


def prepare_points(left_ref, points_ref, right_ref, ln_ref, rn_ref):
    norms_of(left_ref, ln_ref)
    norms_of(points_ref, rn_ref)
    transpose_points(points_ref, right_ref)


def combine(parts):
    peak = jnp.max(parts, axis=0)
    return peak + jnp.log(jnp.sum(jnp.exp(parts - peak[None]), axis=0))


def in_range(total):
    return jnp.logical_and(jnp.min(total) >= smallest, jnp.max(total) <= largest)


class Static:
    def __init__(self, blocks, tiles):
        self.blocks, self.tiles = blocks, tiles

    def each(self, step, unroll=1, tail=1):
        for b in range(self.blocks):
            for k in range(self.tiles):
                step(b, k, b, k)


class Listed:
    def __init__(self, list_ref, blocks, tiles):
        self.list_ref, self.blocks, self.tiles = list_ref, blocks, tiles
        self.room = (list_ref.shape[0] - 1) // 2

    def each(self, step, unroll=1, tail=1):
        def one(pair):
            b = self.list_ref[pair]
            k = self.list_ref[self.room + pair]
            step(jnp.minimum(b, self.blocks - 1), jnp.minimum(k, self.tiles - 1), b, k)

        def groups(first, last, size, start):
            def group(index, carry):
                for u in range(size):
                    one(start + index * size + u)
                return carry

            lax.fori_loop(first, last, group, 0)

        count = self.list_ref[2 * self.room]
        whole = lax.div(count, unroll)
        groups(0, whole, unroll, 0)
        if unroll > tail:
            start = whole * unroll
            groups(0, lax.div(count - start + tail - 1, tail), tail, start)


def at(index, size):
    if isinstance(index, int):
        return pl.ds(index * size, size)
    return pl.ds(pl.multiple_of(index * size, size), size)


def inner_of(right_ref, left_ref, b, k):
    dim = left_ref.shape[0]
    return jnp.dot(
        right_ref[at(k, TILE), :][:, :dim], left_ref[:, at(b, TILE)], preferred_element_type=f32
    )


def half(x, h):
    return x[:, h * LANES : (h + 1) * LANES]


def by_eights(x, op):
    return op(x.reshape(x.shape[0] // 8, 8, x.shape[1]), axis=0)


def row_of(ref, b, h):
    return ref[pl.ds(b * HALVES + h, 1), :]


def gather_columns(acc_ref, tiles, out_ref, op):
    for k in range(tiles):
        for h in range(HALVES):
            part = acc_ref[k, h * LANES : (h + 1) * LANES, :].T
            row = k * HALVES + h
            out_ref[row : row + 1, :] = op(part, axis=0, keepdims=True)


def gather_rows(acc_ref, blocks, out_ref, op):
    for b in range(blocks):
        part = op(acc_ref[b], axis=0, keepdims=True)
        for h in range(HALVES):
            row = b * HALVES + h
            out_ref[row : row + 1, :] = half(part, h)


def col_scores(
    weight, pot, left_norm, right_norm, right_ref, left_ref, pairs, scr, out_ref
):
    dim = left_ref.shape[0]
    scale = 1.0 / (dim * eps)
    vec_ref, vec2_ref, _, _, acc_ref, col_ref, col2_ref = scr
    terms = weight + pot * (1.0 / eps)
    alpha = (terms - left_norm * (0.5 * scale)) * log2e
    top = jnp.max(alpha, keepdims=True)
    alpha = alpha - top
    rows = alpha.shape[0]
    acc_ref[...] = jnp.zeros(acc_ref.shape, f32)

    def add(b, k, to_b, to_k):
        z = inner_of(right_ref, left_ref, b, k) * (scale * log2e)
        parts = [jnp.exp2(half(z, h) + row_of(vec_ref, b, h)) for h in range(HALVES)]
        acc_ref[to_k] += functools.reduce(jnp.add, parts)

    vec_ref[0:rows, :] = alpha
    pairs.each(add, UNROLL, TAIL)
    gather_columns(acc_ref, pairs.tiles, out_ref, jnp.sum)
    total = out_ref[...]
    out_ref[...] = jnp.log(total) + top * ln2 - right_norm * (0.5 * scale)

    @pl.when(jnp.logical_not(in_range(total)))
    def _():
        vec_ref[0:rows, :] = terms
        vec2_ref[0:rows, :] = left_norm
        to_columns(right_norm, col_ref)
        acc_ref[...] = jnp.full(acc_ref.shape, very_low, f32)

        def scores(b, k):
            z = inner_of(right_ref, left_ref, b, k)
            tgt = col_ref[at(k, TILE), :]
            for h in range(HALVES):
                cost = (row_of(vec2_ref, b, h) + tgt - 2.0 * half(z, h)) * (1.0 / (2.0 * dim))
                yield row_of(vec_ref, b, h) - cost * (1.0 / eps)

        def highest(b, k, to_b, to_k):
            acc_ref[to_k] = functools.reduce(jnp.maximum, scores(b, k), acc_ref[to_k])

        pairs.each(highest)
        gather_columns(acc_ref, pairs.tiles, out_ref, jnp.max)
        peak = out_ref[...]
        to_columns(peak, col2_ref)
        acc_ref[...] = jnp.zeros(acc_ref.shape, f32)

        def add_exact(b, k, to_b, to_k):
            peaks = col2_ref[at(k, TILE), :]
            parts = [jnp.exp(s - peaks) for s in scores(b, k)]
            acc_ref[to_k] += functools.reduce(jnp.add, parts)

        pairs.each(add_exact)
        gather_columns(acc_ref, pairs.tiles, out_ref, jnp.sum)
        out_ref[...] = peak + jnp.log(out_ref[...])


def row_scores(
    weight, pot, right_norm, left_norm, right_ref, left_ref, pairs, scr, out_ref
):
    dim = left_ref.shape[0]
    scale = 1.0 / (dim * eps)
    vec_ref, vec2_ref, acc_ref, _, _, col_ref, col2_ref = scr
    terms = weight + pot * (1.0 / eps)
    beta = (terms - right_norm * (0.5 * scale)) * log2e
    top = jnp.max(beta, keepdims=True)
    beta = beta - top
    acc_ref[...] = jnp.zeros(acc_ref.shape, f32)

    def add(b, k, to_b, to_k):
        z = inner_of(right_ref, left_ref, b, k) * (scale * log2e)
        tgt = col_ref[at(k, TILE), :]
        for h in range(HALVES):
            part = by_eights(jnp.exp2(half(z, h) + tgt), jnp.sum)
            acc_ref[to_b, :, h * LANES : (h + 1) * LANES] += part

    to_columns(beta, col_ref)
    pairs.each(add, UNROLL, TAIL)
    gather_rows(acc_ref, pairs.blocks, out_ref, jnp.sum)
    total = out_ref[...]
    out_ref[...] = jnp.log(total) + top * ln2 - left_norm * (0.5 * scale)

    @pl.when(jnp.logical_not(in_range(total)))
    def _():
        rows = left_norm.shape[0]
        to_columns(terms, col_ref)
        to_columns(right_norm, col2_ref)
        vec_ref[0:rows, :] = left_norm
        acc_ref[...] = jnp.full(acc_ref.shape, very_low, f32)

        def scores(b, k):
            z = inner_of(right_ref, left_ref, b, k)
            for h in range(HALVES):
                cost = (row_of(vec_ref, b, h) + col2_ref[at(k, TILE), :] - 2.0 * half(z, h)) * (
                    1.0 / (2.0 * dim)
                )
                yield col_ref[at(k, TILE), :] - cost * (1.0 / eps)

        def highest(b, k, to_b, to_k):
            for h, s in enumerate(scores(b, k)):
                where = slice(h * LANES, (h + 1) * LANES)
                acc_ref[to_b, :, where] = jnp.maximum(
                    acc_ref[to_b, :, where], by_eights(s, jnp.max)
                )

        pairs.each(highest)
        gather_rows(acc_ref, pairs.blocks, out_ref, jnp.max)
        peak = out_ref[...]
        vec2_ref[0:rows, :] = peak
        acc_ref[...] = jnp.zeros(acc_ref.shape, f32)

        def add_exact(b, k, to_b, to_k):
            for h, s in enumerate(scores(b, k)):
                where = slice(h * LANES, (h + 1) * LANES)
                acc_ref[to_b, :, where] += by_eights(
                    jnp.exp(s - row_of(vec2_ref, b, h)), jnp.sum
                )

        pairs.each(add_exact)
        gather_rows(acc_ref, pairs.blocks, out_ref, jnp.sum)
        out_ref[...] = peak + jnp.log(out_ref[...])


def look_up(table, which, out_ref):
    table = table.T
    high = table.astype(bf16)
    rest = table - high.astype(f32)
    middle = rest.astype(bf16)
    low = (rest - middle.astype(f32)).astype(bf16)
    upper = jnp.concatenate([high, middle], axis=1)
    place = lax.broadcasted_iota(jnp.int32, (LANES, TILE), 0)
    for row in range(0, which.shape[0], HALVES):
        index = jnp.concatenate([which[row + h : row + h + 1, :] for h in range(HALVES)], axis=1)
        hot = jnp.where(place == lax.shift_right_logical(index, 7), 1.0, 0.0).astype(bf16)
        value = jnp.dot(upper, jnp.concatenate([hot, hot], axis=0), preferred_element_type=f32)
        value = value + jnp.dot(low, hot, preferred_element_type=f32)
        value = jnp.where(place == jnp.bitwise_and(index, LANES - 1), value, 0.0)
        value = jnp.sum(value, axis=0, keepdims=True)
        for h in range(HALVES):
            out_ref[row + h : row + h + 1, :] = half(value, h)


def to_all(out_ref, value, start=0):
    out_ref[:, start : start + value.shape[0], :] = jnp.broadcast_to(
        value[None], (out_ref.shape[0],) + value.shape
    )


def coarse_start(src_ref, tgt_ref, from_ref, send_ref, *scr):
    *scr, out_ref, left_ref, points_ref, weight_ref, right_ref, ln_ref, rn_ref, sems = scr
    moves = ((src_ref, left_ref), (tgt_ref, points_ref), (from_ref, weight_ref))
    copies = [pltpu.make_async_copy(a, b, sems.at[i]) for i, (a, b) in enumerate(moves)]
    for copy in copies:
        copy.start()
    for copy in copies:
        copy.wait()
    prepare_points(left_ref, points_ref, right_ref, ln_ref, rn_ref)
    pairs = Static(left_ref.shape[1] // TILE, points_ref.shape[1] // TILE)
    weight = weight_ref[...]
    pot = jnp.zeros(weight.shape, f32)
    col_scores(weight, pot, ln_ref[...], rn_ref[...], right_ref, left_ref, pairs, scr, out_ref)
    to_all(send_ref, out_ref[...])


def coarse_rows_first(
    src_ref, points_ref, from_ref, left_ref, right_ref, ln_ref, rn_ref, weight_ref, out_ref, *scr
):
    left_ref[...] = src_ref[...]
    prepare_points(left_ref, points_ref, right_ref, ln_ref, rn_ref)
    weight = from_ref[...]
    weight_ref[...] = weight
    pairs = Static(left_ref.shape[1] // TILE, right_ref.shape[0] // TILE)
    pot = jnp.zeros(weight.shape, f32)
    row_scores(weight, pot, rn_ref[...], ln_ref[...], right_ref, left_ref, pairs, scr, out_ref)


def coarse_rows_second(
    recv_ref, first_ref, left_ref, right_ref, ln_ref, rn_ref, weight_ref, send_ref, tgt_ref, *scr
):
    *scr, out_ref = scr
    tgt = (-0.5 * eps) * combine(recv_ref[...])
    tgt_ref[...] = tgt
    pairs = Static(left_ref.shape[1] // TILE, right_ref.shape[0] // TILE)
    row_scores(
        weight_ref[...], tgt, rn_ref[...], ln_ref[...], right_ref, left_ref, pairs, scr, out_ref
    )
    first = first_ref[...]
    to_all(send_ref, first)
    to_all(send_ref, out_ref[...], first.shape[0])


def coarse_cols(
    recv_ref, left_ref, right_ref, ln_ref, rn_ref, weight_ref, after_ref, send_ref, *scr
):
    *scr, out_ref = scr
    lse = combine(recv_ref[...])
    rows = lse.shape[0] // 2
    first = (-0.5 * eps) * lse[:rows]
    second = 0.5 * (first - eps * lse[rows:])
    to_all(send_ref, second)
    pairs = Static(left_ref.shape[1] // TILE, right_ref.shape[0] // TILE)
    col_scores(
        weight_ref[...], first, ln_ref[...], rn_ref[...], right_ref, left_ref, pairs, scr, out_ref
    )
    to_all(send_ref, out_ref[...], rows)


def coarse_end(recv_ref, tgt_ref, send_ref):
    count = tgt_ref.shape[0]
    rows = recv_ref.shape[1] - count
    lse = combine(recv_ref[:, rows:, :])
    to_all(send_ref, 0.5 * (tgt_ref[...] - eps * lse))


def prepare(
    left_ref, points_ref, support_ref, counts_ref, after_ref, right_ref, ln_ref, rn_ref, list_ref
):
    blocks = left_ref.shape[1] // TILE
    tiles = points_ref.shape[1] // TILE
    most = support_ref.shape[2]
    room = (list_ref.shape[0] - 1) // 2

    def one_block(b, found):
        count = counts_ref[b, 0]
        for m in range(most):
            list_ref[found] = b
            list_ref[room + found] = support_ref[b, 0, m]
            found = found + jnp.where(m < count, 1, 0)
        return found

    found = lax.fori_loop(0, blocks, one_block, 0)
    for u in range(TAIL):
        list_ref[found + u] = blocks
        list_ref[room + found + u] = tiles
    list_ref[2 * room] = found
    prepare_points(left_ref, points_ref, right_ref, ln_ref, rn_ref)


def fine_cols_first(
    list_ref, recv_ref, which_ref, left_ref, right_ref, ln_ref, rn_ref, weight_ref, send_ref, src_ref, *scr
):
    *scr, table_ref, out_ref = scr
    shards = recv_ref.shape[0]
    rows = table_ref.shape[0] // shards
    for shard in range(shards):
        table_ref[shard * rows : (shard + 1) * rows, :] = recv_ref[shard, 0:rows, :]
    look_up(table_ref[...], which_ref[...], src_ref)
    pairs = Listed(list_ref, left_ref.shape[1] // TILE, right_ref.shape[0] // TILE)
    col_scores(
        weight_ref[...], src_ref[...], ln_ref[...], rn_ref[...], right_ref, left_ref, pairs, scr, out_ref
    )
    to_all(send_ref, out_ref[...])


def fine_rows_first(
    list_ref, recv_ref, which_ref, left_ref, right_ref, ln_ref, rn_ref, weight_ref, out_ref, tgt_ref, *scr
):
    *scr, table_ref = scr
    shards = recv_ref.shape[0]
    rows = table_ref.shape[0] // shards
    for shard in range(shards):
        table_ref[shard * rows : (shard + 1) * rows, :] = recv_ref[shard]
    look_up(table_ref[...], which_ref[...], tgt_ref)
    pairs = Listed(list_ref, left_ref.shape[1] // TILE, right_ref.shape[0] // TILE)
    row_scores(
        weight_ref[...], tgt_ref[...], rn_ref[...], ln_ref[...], right_ref, left_ref, pairs, scr, out_ref
    )


def fine_rows_second(
    list_ref, recv_ref, tgt_ref, first_ref, left_ref, right_ref, ln_ref, rn_ref, weight_ref, send_ref, new_ref, *scr
):
    *scr, out_ref = scr
    new_ref[...] = 0.5 * (tgt_ref[...] - eps * combine(recv_ref[...]))
    pairs = Listed(list_ref, left_ref.shape[1] // TILE, right_ref.shape[0] // TILE)
    row_scores(
        weight_ref[...], new_ref[...], rn_ref[...], ln_ref[...], right_ref, left_ref, pairs, scr, out_ref
    )
    shards, rows, _ = send_ref.shape
    rows = rows // 2
    for shard in range(shards):
        where = slice(shard * rows, (shard + 1) * rows)
        send_ref[shard, 0:rows, :] = first_ref[where, :]
        send_ref[shard, rows : 2 * rows, :] = out_ref[where, :]


def combine_rows(recv_ref, send_ref):
    to_all(send_ref, combine(recv_ref[...]))


def fine_cols_second(
    list_ref, recv_ref, src_ref, left_ref, right_ref, ln_ref, rn_ref, weight_ref, send_ref, *scr
):
    *scr, first_ref, out_ref = scr
    shards, rows, _ = recv_ref.shape
    rows = rows // 2
    for shard in range(shards):
        where = slice(shard * rows, (shard + 1) * rows)
        first_ref[where, :] = 0.5 * (src_ref[where, :] - eps * recv_ref[shard, 0:rows, :])
    pairs = Listed(list_ref, left_ref.shape[1] // TILE, right_ref.shape[0] // TILE)
    col_scores(
        weight_ref[...], first_ref[...], ln_ref[...], rn_ref[...], right_ref, left_ref, pairs, scr, out_ref
    )
    to_all(send_ref, out_ref[...])


def fine_end(rows_ref, src_ref, recv_ref, tgt_ref, src_out_ref, tgt_out_ref):
    shards, rows, _ = rows_ref.shape
    rows = rows // 2
    for shard in range(shards):
        where = slice(shard * rows, (shard + 1) * rows)
        first = 0.5 * (src_ref[where, :] - eps * rows_ref[shard, 0:rows, :])
        src_out_ref[where, :] = 0.5 * (first - eps * rows_ref[shard, rows : 2 * rows, :])
    tgt_out_ref[...] = 0.5 * (tgt_ref[...] - eps * combine(recv_ref[...]))


def scratch_for(left, right, spare):
    rows = left // LANES
    return [
        pltpu.VMEM((rows, LANES), f32),
        pltpu.VMEM((rows, LANES), f32),
        pltpu.VMEM((left // TILE + spare, 8, TILE), f32),
        pltpu.VMEM((8, LANES), f32),
        pltpu.VMEM((right // TILE + spare, TILE, LANES), f32),
        pltpu.VMEM((right, LANES), f32),
        pltpu.VMEM((right, LANES), f32),
    ]


def call(body, outs, operands, scratch=(), smem=(), smem_out=(), hbm=(), work=0, limit=24):
    spaces = [
        pltpu.SMEM if i in smem else pltpu.HBM if i in hbm else pltpu.VMEM for i in range(len(operands))
    ]
    out_spaces = [pltpu.SMEM if i in smem_out else pltpu.VMEM for i in range(len(outs))]
    return pl.pallas_call(
        body,
        out_shape=[jax.ShapeDtypeStruct(shape, dtype) for shape, dtype in outs],
        in_specs=[pl.BlockSpec(memory_space=s) for s in spaces],
        out_specs=[pl.BlockSpec(memory_space=s) for s in out_spaces],
        scratch_shapes=list(scratch),
        compiler_params=pltpu.CompilerParams(vmem_limit_bytes=limit * 1024 * 1024),
        cost_estimate=pl.CostEstimate(
            flops=128 * work + 1000, bytes_accessed=1 << 20, transcendentals=work
        ),
    )(*operands)


def exchange(x, axis):
    return lax.all_to_all(x, axis, 0, 0, tiled=True)


def per_device(
    n_src,
    n_tgt,
    src_centroids,
    tgt_centroids,
    src_weights,
    tgt_weights,
    src_cells,
    tgt_cells,
    src_mass,
    tgt_mass,
    src_cluster,
    tgt_cluster,
    support,
    counts,
):
    cs, ct = src_centroids.shape[1], tgt_centroids.shape[1]
    fs, ft = src_cells.shape[1], tgt_cells.shape[1]
    csr, ctr, fsr, ftr = (n // LANES for n in (cs, ct, fs, ft))
    vec = lambda x: x.reshape(-1, LANES)
    src_weights, tgt_weights, src_mass, tgt_mass, src_cluster, tgt_cluster = map(
        vec, (src_weights, tgt_weights, src_mass, tgt_mass, src_cluster, tgt_cluster)
    )
    coarse_scratch = scratch_for(cs, ct, 0)
    fine_scratch = scratch_for(fs, ft, 1)
    one = lambda rows: pltpu.VMEM((rows, LANES), f32)
    coarse_work = cs * ct
    fine_work = fs * ft // 4

    (send,) = call(
        coarse_start,
        [((n_src, ctr, LANES), f32)],
        [src_centroids, tgt_centroids, src_weights],
        coarse_scratch
        + [
            one(ctr),
            pltpu.VMEM(src_centroids.shape, bf16),
            pltpu.VMEM(tgt_centroids.shape, bf16),
            one(csr),
            pltpu.VMEM((ct, LANES), bf16),
            one(csr),
            one(ctr),
            pltpu.SemaphoreType.DMA((3,)),
        ],
        hbm=(0, 1, 2),
        limit=64,
        work=coarse_work,
    )
    recv = exchange(send, "src")
    left, right, ln, rn, tgt_weights, first_rows = call(
        coarse_rows_first,
        [
            (src_centroids.shape, bf16),
            ((ct, LANES), bf16),
            ((csr, LANES), f32),
            ((ctr, LANES), f32),
            ((ctr, LANES), f32),
            ((csr, LANES), f32),
        ],
        [src_centroids, tgt_centroids, tgt_weights],
        coarse_scratch,
        work=coarse_work,
    )
    send, coarse_tgt = call(
        coarse_rows_second,
        [((n_tgt, 2 * csr, LANES), f32), ((ctr, LANES), f32)],
        [recv, first_rows, left, right, ln, rn, tgt_weights],
        coarse_scratch + [one(csr)],
        work=coarse_work,
    )
    room = support.shape[0] * support.shape[2] + TAIL
    fine_right, fine_ln, fine_rn, listed = call(
        prepare,
        [
            ((ft, LANES), bf16),
            ((fsr, LANES), f32),
            ((ftr, LANES), f32),
            ((2 * room + 1,), jnp.int32),
        ],
        [src_cells, tgt_cells, support, counts, coarse_tgt],
        smem=(2, 3),
        smem_out=(3,),
        work=2 * coarse_work,
    )
    recv = exchange(send, "tgt")
    (send,) = call(
        coarse_cols,
        [((n_src, csr + ctr, LANES), f32)],
        [recv, left, right, ln, rn, src_weights, fine_rn],
        coarse_scratch + [one(ctr)],
        work=coarse_work,
    )
    every_src = exchange(send, "src")
    (send,) = call(coarse_end, [((n_tgt, ctr, LANES), f32)], [every_src, coarse_tgt])
    every_tgt = exchange(send, "tgt")

    fine_static = [src_cells, fine_right, fine_ln, fine_rn]
    send, fine_src = call(
        fine_cols_first,
        [((n_src, ftr, LANES), f32), ((fsr, LANES), f32)],
        [listed, every_src, src_cluster, *fine_static, src_mass],
        fine_scratch + [one(n_src * csr), one(ftr)],
        smem=(0,),
        work=fine_work,
    )
    recv = exchange(send, "src")
    first_rows, fine_tgt = call(
        fine_rows_first,
        [((fsr, LANES), f32), ((ftr, LANES), f32)],
        [listed, every_tgt, tgt_cluster, *fine_static, tgt_mass],
        fine_scratch + [one(n_tgt * ctr)],
        smem=(0,),
        work=fine_work,
    )
    send, fine_tgt = call(
        fine_rows_second,
        [((n_tgt, 2 * fsr // n_tgt, LANES), f32), ((ftr, LANES), f32)],
        [listed, recv, fine_tgt, first_rows, *fine_static, tgt_mass],
        fine_scratch + [one(fsr)],
        smem=(0,),
        work=fine_work,
    )
    recv = exchange(send, "tgt")
    (send,) = call(combine_rows, [(recv.shape, f32)], [recv])
    rows = exchange(send, "tgt")
    (send,) = call(
        fine_cols_second,
        [((n_src, ftr, LANES), f32)],
        [listed, rows, fine_src, *fine_static, src_mass],
        fine_scratch + [one(fsr), one(ftr)],
        smem=(0,),
        work=fine_work,
    )
    recv = exchange(send, "src")
    fine_src, fine_tgt = call(
        fine_end,
        [((fsr, LANES), f32), ((ftr, LANES), f32)],
        [rows, fine_src, recv, fine_tgt],
    )
    return (fine_src.reshape(fs), fine_tgt.reshape(ft))


def solution(mesh):
    in_specs = (
        P(None, "src"),
        P(None, "tgt"),
        P("src"),
        P("tgt"),
        P(None, "src"),
        P(None, "tgt"),
        P("src"),
        P("tgt"),
        P("src"),
        P("tgt"),
        P("src", "tgt", None),
        P("src", "tgt"),
    )
    out_specs = (P("src"), P("tgt"))
    body = functools.partial(per_device, mesh.shape["src"], mesh.shape["tgt"])
    return jax.shard_map(body, mesh=mesh, in_specs=in_specs, out_specs=out_specs, check_vma=False)
```
